32 devices in a mesh: ctx: 8 (over z, x), exp: 4 (over y, core).
Axes of the slice: x: 2, y: 2, z: 4, core: 2. Of those that a mesh axis runs over, the one named last changes fastest.
Arguments:
- tokens: bfloat16 [2048, 2880], P('ctx', 'exp'), may hold values from -6 to 6
- cotangent: bfloat16 [2048, 2880], P('ctx', 'exp'), may hold values from -4 to 4
- expert_indices: int32 [2048, 4], P('ctx'), may hold values from 0 to 127, all different within a row; in each aligned block of 256 rows (0 to 255, 256 to 511, ...) at most 16 rows name the same one
- routing_weights: float32 [2048, 4], P('ctx'), may hold values from 0.2 to 1
- gate_up_weight_blocks: bfloat16 [8, 2, 2880, 2880], P('ctx', None, 'exp'), may hold values from -6 to 6
- gate_up_block_scales: float32 [8, 2, 2880, 90], P('ctx', None, 'exp'), may hold values from 0.01 to 0.1
- down_weight_blocks: bfloat16 [8, 2880, 2880], P('ctx', 'exp'), may hold values from -6 to 6
- down_block_scales: float32 [8, 2880, 90], P('ctx', 'exp'), may hold values from 0.002 to 0.008
- adapter_down_matrix: bfloat16 [8, 2880, 16], P('ctx', 'exp'), may hold values from -0.109375 to 0.109375
- adapter_up_matrix: bfloat16 [8, 16, 2880], P('ctx', None, 'exp'), may hold values from -1.5 to 1.5
Outputs:
- moe_out: bfloat16 [2048, 2880], P('ctx', 'exp')
- left_gradient: float32 [8, 2880, 16], P('ctx', 'exp')
- right_gradient: float32 [8, 16, 2880], P('ctx', None, 'exp')
The draws below stay inside these ranges and needn't reach their ends.
Inputs may be any that keep to these rules, and one draw needn't show every extreme that they name: `expert_indices`: each row names 4 different experts. Within the 256 rows of one index of ctx no expert is named more than 16 times, a bound that some block reaches.
All inputs are finite; a program needn't handle non-finite values.
Results may differ from the reference program's by a relative error of at most 0.018.
Values may be sent and summed in bfloat16 or wider, within the bound.
A program may use at most 64 MiB of HBM per device.

```python
import math
from functools import partial
import jax
import jax.numpy as jnp
import numpy as np
from jax import lax

MODEL_WIDTH = 2880
HIDDEN_UNITS = 2880
EXPERTS = 128
TOP = 4
ADAPTER_RANK = 16
TOK_DEV = 256
TOKENS = 2048
CAP = 16
EXPERTS_ACTIVE = 8
N_CTX = 8
N_EXP = 4


def spiked(entries, key, source, target, shards_of, factor):
    def block_of(axis_at):
        return (jnp.arange(entries.shape[axis_at]) // (entries.shape[axis_at] // shards_of)).reshape((-1,) + (1,) * (entries.ndim - 1 - axis_at))

    one_side = jax.random.permutation(key, shards_of)[block_of(target)]
    second = (block_of(target) + shards_of // 2) % shards_of
    return jnp.where((block_of(source) == one_side) | (block_of(source) == second), factor * entries, entries)


def steps_of(stream_key, extent, cuts, low, high):
    def one(axis_at, parts):
        steps = jax.random.uniform(jax.random.fold_in(jax.random.fold_in(stream_key, 6), axis_at), (parts,), jnp.float32, low / len(cuts), high / len(cuts))
        return jnp.repeat(jnp.exp(steps), extent[axis_at] // parts).reshape((-1,) + (1,) * (len(extent) - axis_at - 1))

    factor_of = one(*cuts[0])
    for cut in cuts[1:]:
        factor_of = factor_of * one(*cut)
    return factor_of


def assign_block(stream_key, own, number, rows, number_of, top, limit, slope):
    ranking = jax.random.permutation(stream_key, number_of)
    crowded, usual = load_shares(number_of, rows * top, limit, slope, True), load_shares(number_of, rows * top, limit, slope, False)
    places = jnp.arange(number_of)

    def named(tallies, turn):
        used = int((tallies > 0).sum())
        fixed = max(1, used // 4)
        moved = fixed + (places - fixed + turn * (used - fixed)) % max(1, number_of - fixed)
        return jnp.zeros((number_of,), jnp.int32).at[ranking[jnp.where(places < fixed, places, moved)]].set(jnp.asarray(tallies, jnp.int32))

    tallies = jnp.where(number % 4 == 0, named(crowded, number // 4), named(usual, number - number // 4 - 1))
    mixed = jax.random.permutation(jax.random.fold_in(own, 3), number_of)
    source_of, taker = mixed[0:number_of // 2 * 2:2], mixed[1:number_of // 2 * 2:2]
    margin = jnp.minimum(tallies[source_of] - 1, limit - tallies[taker]) // 2
    margin = jnp.where((source_of == ranking[0]) | (taker == ranking[0]) | (tallies[taker] == 0), 0, jnp.maximum(margin, 0))
    moved = jax.random.randint(jax.random.fold_in(own, 4), (number_of // 2,), 0, 1 << 20) % (margin + 1)
    tallies = tallies.at[source_of].add(-moved).at[taker].add(moved)
    members = jnp.searchsorted(jnp.cumsum(tallies), jnp.arange(rows * top), side="right").astype(jnp.int32)
    grid = members.reshape(top, rows).T
    grid = grid[jax.random.permutation(jax.random.fold_in(own, 1), rows)]
    turn = jax.random.randint(jax.random.fold_in(own, 2), (rows, 1), 0, top)
    return jnp.take_along_axis(grid, (jnp.arange(top)[None, :] + turn) % top, axis=1)


def load_shares(number_of, total, limit, slope, full):
    loads = [(1 << 20) // math.isqrt(standing ** slope) + 1 for standing in range(1, number_of + 1)]
    largest = limit if full else min(limit, max(-(-total // number_of), total * loads[0] // sum(loads)))
    least = 1 if total - largest >= number_of - 1 else 0
    counts, surplus = [largest] + [least] * (number_of - 1), total - largest - least * (number_of - 1)
    while surplus > 0:
        movable = [i for i in range(1, number_of) if counts[i] < largest] or [i for i in range(1, number_of) if counts[i] < limit]
        mass, budget = sum([loads[i] for i in movable]), surplus
        for i in movable:
            addition = min(limit - counts[i], max(1, budget * loads[i] // mass), surplus)
            counts[i] = counts[i] + addition
            surplus = surplus - addition
    return np.array(counts)


def normal_values(key, shape, scale, reach, cuts=(), kind=jnp.bfloat16):
    array = jax.random.normal(key, shape, jnp.float32) * scale
    if len(cuts) > 0:
        array = steps_of(key, shape, cuts, -0.22, 0.18) * array
    return jnp.clip(array, min=-reach, max=reach).astype(kind)


def noise_with(key, extent, scale, limit, shards, heavy, held_as=jnp.bfloat16):
    result = scale * jax.random.normal(key, extent, jnp.float32)
    if shards:
        result = result * steps_of(key, extent, shards, -0.22, 0.18)
    return jnp.clip(spiked(result, jax.random.fold_in(key, 3), *heavy), -limit, limit).astype(held_as)


def setup_inputs(seed: int = 0) -> dict:
    splits = jax.random.split(jax.random.key(seed), 11)
    tokens = normal_values(splits[0], (TOKENS, MODEL_WIDTH), 1.0, 6.0, ((0, 8), (1, 4)))
    cotangent = normal_values(splits[1], (TOKENS, MODEL_WIDTH), 0.25, 4.0, ((0, 8), (1, 4)))
    expert_indices_keys = jax.random.split(jax.random.fold_in(splits[2], 1), TOKENS // TOK_DEV)
    expert_indices_turns = jax.random.permutation(jax.random.fold_in(splits[2], 3), TOKENS // TOK_DEV)
    expert_indices = jax.vmap(lambda own, number: assign_block(jax.random.fold_in(splits[2], 2), own, number, TOK_DEV, EXPERTS, TOP, CAP, 2))(expert_indices_keys, expert_indices_turns).reshape((TOKENS, TOP))
    routing_weights = jnp.clip(0.2 + 0.8 * jax.random.uniform(splits[3], (TOKENS, TOP), jnp.float32) ** steps_of(splits[3], (TOKENS, TOP), ((0, 8),), -0.2, 0.2), 0.2, 1.0)
    gate_up_weight_blocks = normal_values(splits[4], (EXPERTS_ACTIVE, 2, HIDDEN_UNITS, MODEL_WIDTH), 1.0, 6.0, ((0, 8), (2, 4)))
    gate_up_block_scales = jnp.clip(jnp.exp(math.log(0.1) - 2.3025851 * jax.random.uniform(splits[5], (EXPERTS_ACTIVE, 2, HIDDEN_UNITS, MODEL_WIDTH // 32), jnp.float32) ** steps_of(splits[5], (EXPERTS_ACTIVE, 2, HIDDEN_UNITS, MODEL_WIDTH // 32), ((0, 8), (2, 4)), -0.2, 0.2)), 0.01, 0.1)
    down_weight_blocks = noise_with(splits[6], (EXPERTS_ACTIVE, HIDDEN_UNITS, MODEL_WIDTH), 1.0, 6.0, ((0, 8), (1, 4)), (1, 2, 4, 2.0))
    down_block_scales = jnp.clip(jnp.exp(math.log(0.008) - 1.3862944 * jax.random.uniform(splits[7], (EXPERTS_ACTIVE, HIDDEN_UNITS, MODEL_WIDTH // 32), jnp.float32) ** steps_of(splits[7], (EXPERTS_ACTIVE, HIDDEN_UNITS, MODEL_WIDTH // 32), ((0, 8), (1, 4)), -0.2, 0.2)), 0.002, 0.008)
    adapter_down_matrix = normal_values(splits[8], (EXPERTS_ACTIVE, HIDDEN_UNITS, ADAPTER_RANK), HIDDEN_UNITS ** -0.5, 0.109375, ((0, 8), (1, 4)))
    adapter_up_matrix = normal_values(splits[9], (EXPERTS_ACTIVE, ADAPTER_RANK, MODEL_WIDTH), ADAPTER_RANK ** -0.5, 1.5, ((0, 8), (2, 4)))
    return dict(tokens=tokens, cotangent=cotangent, expert_indices=expert_indices, routing_weights=routing_weights, gate_up_weight_blocks=gate_up_weight_blocks, gate_up_block_scales=gate_up_block_scales, down_weight_blocks=down_weight_blocks, down_block_scales=down_block_scales, adapter_down_matrix=adapter_down_matrix, adapter_up_matrix=adapter_up_matrix)


ADAPTER_SCALE = 0.5
GLU_ALPHA = 1.702
CLAMP_LIMIT = 7.0


def slot_table(expert_indices, flight, capacity):
    flat_ids = expert_indices.reshape(-1)
    onehot = (flat_ids[:, None] == jnp.arange(flight, dtype=jnp.int32)[None, :]).astype(jnp.int32)
    before = jnp.cumsum(onehot, axis=0) - onehot
    position = jnp.sum(before * onehot, axis=1)
    is_live = jnp.sum(onehot, axis=1) > 0
    target = jnp.where(is_live, flat_ids * capacity + position, -1)
    return target.reshape(expert_indices.shape).astype(jnp.int32)


def slot_sources(target, slot_count):
    flat_target = target.reshape(-1)
    matches = flat_target[None, :] == jnp.arange(slot_count, dtype=jnp.int32)[:, None]
    pair_index = jnp.arange(flat_target.shape[0], dtype=jnp.int32)
    chosen = jnp.sum(jnp.where(matches, pair_index[None, :], 0), axis=1).astype(jnp.int32)
    filled = jnp.any(matches, axis=1)
    return chosen, filled


def dispatch_rows(tokens, cotangent, routing_weights, chosen, filled, choices):
    token_of = chosen // choices
    weight_of = jnp.where(filled, routing_weights.reshape(-1)[chosen], 0.0)
    row_data = jnp.where(filled[:, None], tokens[token_of], jnp.zeros((), tokens.dtype))
    gradient_rows = (weight_of[:, None] * cotangent[token_of].astype(jnp.float32)).astype(jnp.bfloat16)
    return row_data, gradient_rows


def combine_rows(table, target, routing_weights):
    safe_index = jnp.maximum(target, 0).reshape(-1)
    picked = table[safe_index].astype(jnp.float32).reshape(target.shape + (table.shape[1],))
    scaled = jnp.where(target >= 0, routing_weights, 0.0)
    return jnp.sum(picked * scaled[:, :, None], axis=1).astype(jnp.bfloat16)


def dequant_gate_up(blocks, scales):
    pair, hidden, width = blocks.shape
    shaped = blocks.astype(jnp.float32).reshape(pair, hidden, width // 32, 32)
    return (shaped * scales[:, :, :, None]).reshape(pair, hidden, width).astype(jnp.bfloat16)


def dequant_down(blocks, scales):
    hidden, width = blocks.shape
    shaped = blocks.astype(jnp.float32).reshape(hidden, width // 32, 32)
    return (shaped * scales[:, :, None]).reshape(hidden, width).astype(jnp.bfloat16)


def glu_activate(gate_part, up_part):
    gate_cut = jnp.minimum(gate_part, CLAMP_LIMIT)
    up_cut = jnp.clip(up_part, -CLAMP_LIMIT, CLAMP_LIMIT)
    return ((up_cut + 1.0) * gate_cut * jax.nn.sigmoid(GLU_ALPHA * gate_cut)).astype(jnp.bfloat16)


def expert_update(operands):
    row_data, gradient_rows, joined_blocks, joined_scales, down_codes, down_factors, adapter_left, adapter_right = operands
    w_joined = dequant_gate_up(joined_blocks, joined_scales)
    w_down = dequant_down(down_codes, down_factors)
    hidden = w_down.shape[0]
    gate_part = jnp.dot(row_data, w_joined[0].T, preferred_element_type=jnp.float32)
    up_part = jnp.dot(row_data, w_joined[1].T, preferred_element_type=jnp.float32)
    activated = glu_activate(gate_part, up_part)
    width_part = hidden // N_EXP
    partial_sums = jnp.einsum("sgh,ghd->gsd", activated.reshape(-1, N_EXP, width_part).astype(jnp.float32), w_down.reshape(N_EXP, width_part, MODEL_WIDTH).astype(jnp.float32))
    rounded = lax.optimization_barrier(partial_sums.astype(jnp.bfloat16))
    frozen_base = jnp.sum(rounded.astype(jnp.float32), axis=0)
    reduced_rank = jnp.dot(activated, adapter_left, preferred_element_type=jnp.float32).astype(jnp.bfloat16)
    expert_output = (frozen_base + ADAPTER_SCALE * jnp.dot(reduced_rank, adapter_right, preferred_element_type=jnp.float32)).astype(jnp.bfloat16)
    right_gradient = ADAPTER_SCALE * jnp.dot(reduced_rank.T, gradient_rows, preferred_element_type=jnp.float32)
    backward_rank = (ADAPTER_SCALE * jnp.dot(gradient_rows, adapter_right.T, preferred_element_type=jnp.float32)).astype(jnp.bfloat16)
    left_gradient = jnp.dot(activated.T, backward_rank, preferred_element_type=jnp.float32)
    return expert_output, left_gradient, right_gradient


def reference(tokens, cotangent, expert_indices, routing_weights, gate_up_weight_blocks, gate_up_block_scales, down_weight_blocks, down_block_scales, adapter_down_matrix, adapter_up_matrix):
    flight = N_CTX
    slot_count = flight * CAP
    id_blocks = expert_indices.reshape(flight, TOK_DEV, TOP)
    weight_blocks = routing_weights.reshape(flight, TOK_DEV, TOP)
    token_blocks = tokens.reshape(flight, TOK_DEV, MODEL_WIDTH)
    cot_blocks = cotangent.reshape(flight, TOK_DEV, MODEL_WIDTH)
    targets = jax.vmap(partial(slot_table, flight=flight, capacity=CAP))(id_blocks)
    chosen, filled = jax.vmap(partial(slot_sources, slot_count=slot_count))(targets)
    row_data, gradient_rows = jax.vmap(partial(dispatch_rows, choices=TOP))(token_blocks, cot_blocks, weight_blocks, chosen, filled)
    per_expert = row_data.reshape(flight, flight, CAP, MODEL_WIDTH).transpose(1, 0, 2, 3).reshape(flight, slot_count, MODEL_WIDTH)
    gradients_per = gradient_rows.reshape(flight, flight, CAP, MODEL_WIDTH).transpose(1, 0, 2, 3).reshape(flight, slot_count, MODEL_WIDTH)
    expert_output, left_gradient, right_gradient = lax.map(expert_update, (per_expert, gradients_per, gate_up_weight_blocks, gate_up_block_scales, down_weight_blocks, down_block_scales, adapter_down_matrix, adapter_up_matrix))
    tables = expert_output.reshape(flight, flight, CAP, MODEL_WIDTH).transpose(1, 0, 2, 3).reshape(flight, slot_count, MODEL_WIDTH)
    moe_out = jax.vmap(combine_rows)(tables, targets, weight_blocks).reshape(TOKENS, MODEL_WIDTH)
    return moe_out, left_gradient, right_gradient
```

```python
import functools

import jax
import jax.numpy as jnp
from jax import lax
from jax.experimental import pallas as pl
from jax.experimental.pallas import tpu as pltpu
from jax.sharding import PartitionSpec as P

CAP = 16
BLOCK = 32
ADAPTER_SCALE = 0.5
GLU_ALPHA = 1.702
CLAMP_LIMIT = 7.0

F32 = jnp.float32
BF16 = jnp.bfloat16
NN = (((1,), (0,)), ((), ()))
NT = (((1,), (1,)), ((), ()))
TN = (((0,), (0,)), ((), ()))


def dot(a, b, dims):
    return lax.dot_general(a, b, dims, preferred_element_type=F32)


def unit_rows(hidden):
    for rows in (240, 144, 128, 80, 48, 16):
        if hidden % rows == 0:
            return rows
    return hidden


def block_kernel(
    C, F,
    tok_h, cot_h, idx_h, rw_h, gu_h, gus_h, dn_h, dns_h, adl_h, adu_h,
    out_h, lg_h, rg_h,
    tok, cot, idx, rw, raw, gus, dns, adl, adu,
    spad, ssc, expand, rows, grows, xin, gin, xfull, wd,
    base, part, pair, tosend, fromy, rank_b, rank_l, outrows, ret,
    out_v, lg_v, rg_v,
    load, store, tS, tR, gS, gR, rS, rR, yS, yR, kS, kR, bS, bR, lS, lR, pS, pR, qS, qR,
):
    NY = F // 2
    H, width = raw.shape[1], raw.shape[2]
    feat = tok.shape[0]
    T = tok.shape[1]
    R = C * CAP
    NB = width // BLOCK
    c = lax.axis_index("ctx")
    f = lax.axis_index("exp")
    y = f // 2
    q = f % 2
    mate = f + 1 - 2 * q

    def at_ctx(other):
        return dict(device_id=(other, f), device_id_type=pl.DeviceIdType.MESH)

    def at_exp(other):
        return dict(device_id=(c, other), device_id_type=pl.DeviceIdType.MESH)

    barrier = pltpu.get_barrier_semaphore()

    @pl.loop(1, C)
    def _(i):
        pl.semaphore_signal(barrier, inc=1, **at_ctx(lax.rem(c + i, C)))

    @pl.loop(1, F)
    def _(i):
        pl.semaphore_signal(barrier, inc=1, **at_exp(lax.rem(f + i, F)))

    loads = [
        pltpu.make_async_copy(idx_h, idx, load.at[0]),
        pltpu.make_async_copy(tok_h, tok, load.at[1]),
        pltpu.make_async_copy(rw_h, rw, load.at[2]),
        pltpu.make_async_copy(cot_h, cot, load.at[3]),
        pltpu.make_async_copy(gus_h, gus, load.at[4]),
        pltpu.make_async_copy(dns_h, dns, load.at[5]),
        pltpu.make_async_copy(gu_h.at[0], raw.at[0], load.at[6]),
        pltpu.make_async_copy(gu_h.at[1], raw.at[1], load.at[7]),
        pltpu.make_async_copy(dn_h, raw.at[2], load.at[8]),
        pltpu.make_async_copy(adl_h, adl, load.at[9]),
        pltpu.make_async_copy(adu_h, adu, load.at[10]),
    ]
    for copy in loads:
        copy.start()

    loads[0].wait()
    slot = lax.broadcasted_iota(jnp.int32, (R, T), 0)
    expert = lax.shift_right_logical(slot, 4)
    number = lax.bitwise_and(slot, 15).astype(F32)
    named = idx[0:1, :] == expert
    for k in range(1, idx.shape[0]):
        named = jnp.logical_or(named, idx[k:k + 1, :] == expert)
    earlier = (
        lax.broadcasted_iota(jnp.int32, (T, T), 0) < lax.broadcasted_iota(jnp.int32, (T, T), 1)
    ).astype(F32).astype(BF16)
    position = dot(named.astype(F32).astype(BF16), earlier, NN)
    hit = jnp.logical_and(named, position == number)
    pick = hit.astype(F32).astype(BF16)
    loads[1].wait()
    rows[...] = dot(pick, tok[...], NT).astype(BF16).reshape(C, CAP, feat)

    pl.semaphore_wait(barrier, C - 1 + F - 1)

    def send_rows(src, dst, ss, rs, other, **where):
        return pltpu.make_async_remote_copy(
            src_ref=src, dst_ref=dst, send_sem=ss, recv_sem=rs, **where
        )

    def tok_copy(other, came):
        return send_rows(rows.at[other], xin.at[f, came], tS.at[other], tR.at[came], other, **at_ctx(other))

    def grad_copy(other, came):
        return send_rows(grows.at[other], gin.at[came], gS.at[other], gR.at[came], other, **at_ctx(other))

    def ret_copy(other, came):
        return send_rows(outrows.at[other], ret.at[came], rS.at[other], rR.at[came], other, **at_ctx(other))

    def y_copy(b, yy, came):
        return send_rows(
            xin.at[2 * came + q, b], xin.at[2 * came + q, b], yS.at[yy, b], yR.at[came, b], 0,
            **at_exp(2 * yy + q),
        )

    def k_copy(yy, b, core):
        return send_rows(
            xin.at[2 * yy + core, b], xin.at[2 * yy + core, b], kS.at[yy, b], kR.at[yy, b], 0,
            **at_exp(mate),
        )

    @pl.loop(1, C)
    def _(i):
        other = lax.rem(c + i, C)
        tok_copy(other, c).start()

    xin[f, c] = rows[c]

    loads[2].wait()
    weight = jnp.zeros((R, T), F32)
    for k in range(idx.shape[0]):
        weight = weight + jnp.where(idx[k:k + 1, :] == expert, rw[k:k + 1, :], 0.0)
    weight = jnp.where(hit, weight, 0.0)
    wd[...] = weight
    loads[3].wait()
    picked = dot(pick, cot[...], NT) * jnp.sum(weight, axis=1, keepdims=True)
    grows[...] = picked.astype(BF16).reshape(C, CAP, feat)

    @pl.loop(1, C)
    def _(i):
        other = lax.rem(c + i, C)
        grad_copy(other, c).start()

    gin[c] = grows[c]

    expand[...] = (
        lax.shift_right_logical(lax.broadcasted_iota(jnp.int32, expand.shape, 1), 5)
        == lax.broadcasted_iota(jnp.int32, expand.shape, 0)
    ).astype(F32).astype(BF16)
    spad[...] = jnp.zeros_like(spad)
    loads[4].wait()
    loads[5].wait()
    for m in range(3):
        if m < 2:
            spad[0:NB, 0:H] = gus[:, m, :]
        else:
            spad[0:NB, 0:H] = dns[:, 0, :]
        ssc[m] = jnp.transpose(spad[...]).astype(BF16)[0:H]
    for i in (6, 7, 8):
        loads[i].wait()

    unit = unit_rows(H)
    per = H // unit
    lanes = 256

    def dequant(u):
        m = u // per
        at = pl.ds(pl.multiple_of(lax.rem(u, per) * unit, unit), unit) if per > 1 else slice(None)
        scale = ssc[m, at, :]
        for lo in range(0, width, lanes):
            hi = min(lo + lanes, width)
            spread = dot(scale, expand[:, lo:hi], NN).astype(BF16)
            raw[m, at, lo:hi] = raw[m, at, lo:hi] * spread

    def forward(i):
        b = lax.rem(c - i + C, C)

        @pl.when(i > 0)
        def _():
            tok_copy(b, b).wait_recv()

        @pl.loop(1, NY)
        def _(j):
            y_copy(b, lax.rem(y + j, NY), y).start()

        k_copy(y, b, q).start()

    units = 3 * per
    groups = -(-C // units)

    @pl.loop(0, units)
    def _(u):
        @pl.loop(0, groups)
        def _(g):
            i = u * groups + g

            @pl.when(i < C)
            def _():
                forward(i)

        dequant(u)

    @pl.loop(1, NY)
    def _(j):
        yy = lax.rem(y - j + NY, NY)

        @pl.loop(0, C)
        def _(i):
            b = lax.rem(c - i + C, C)
            y_copy(b, y, yy).wait_recv()
            k_copy(yy, b, q).start()

    @pl.loop(1, C)
    def _(i):
        b = lax.rem(c - i + C, C)
        grad_copy(b, b).wait_recv()

    loads[9].wait()
    loads[10].wait()
    grads = gin[...].reshape(R, feat)
    right = adu[...]
    rank_b[f] = dot(right, grads, NT).astype(BF16)

    def rank_copy(buf, ss, rs, other, came):
        return send_rows(buf.at[came], buf.at[came], ss.at[other], rs.at[came], other, **at_exp(other))

    @pl.loop(1, F)
    def _(j):
        rank_copy(rank_b, bS, bR, lax.rem(f + j, F), f).start()

    @pl.loop(0, NY)
    def _(yy):
        @pl.loop(0, C)
        def _(b):
            k_copy(yy, b, 1 - q).wait_recv()

    for g in range(F):
        xfull[:, g * feat:(g + 1) * feat] = xin[g].reshape(R, feat)
    x = xfull[...]
    gate = jnp.minimum(dot(x, raw[0], NT), CLAMP_LIMIT)
    up = jnp.clip(dot(x, raw[1], NT), -CLAMP_LIMIT, CLAMP_LIMIT)
    activated = ((up + 1.0) * gate / (1.0 + jnp.exp(-GLU_ALPHA * gate))).astype(BF16)

    rank_l[f] = dot(adl[...], activated, NT).astype(BF16)

    @pl.loop(1, F)
    def _(j):
        rank_copy(rank_l, lS, lR, lax.rem(f + j, F), f).start()

    base[...] = dot(activated, raw[2], NN)
    for g in range(F):
        part[g] = base[:, g * feat:(g + 1) * feat].astype(BF16)

    def pair_copy(yy, core):
        return send_rows(
            part.at[2 * yy + core], pair.at[yy], pS.at[yy], pR.at[yy], 0, **at_exp(mate)
        )

    def sum_copy(yy, came):
        return send_rows(tosend.at[yy], fromy.at[came], qS.at[yy], qR.at[came], 0, **at_exp(2 * yy + q))

    @pl.loop(1, NY + 1)
    def _(j):
        pair_copy(lax.rem(y + j, NY), 1 - q).start()

    @pl.loop(1, NY)
    def _(j):
        yy = lax.rem(y + j, NY)
        pair_copy(yy, q).wait_recv()
        tosend[yy] = (part[2 * yy + q].astype(F32) + pair[yy].astype(F32)).astype(BF16)
        sum_copy(yy, y).start()

    @pl.loop(1, F)
    def _(j):
        other = lax.rem(f - j + F, F)
        rank_copy(rank_b, bS, bR, other, other).wait_recv()
        rank_copy(rank_l, lS, lR, other, other).wait_recv()

    low = rank_l[0].astype(F32)
    back = rank_b[0].astype(F32)
    for g in range(1, F):
        low = low + rank_l[g].astype(F32)
        back = back + rank_b[g].astype(F32)
    low = low.astype(BF16)
    back = (ADAPTER_SCALE * back).astype(BF16)
    lg_v[...] = dot(back, activated, NN)
    rg_v[...] = ADAPTER_SCALE * dot(low, grads, NN)
    pltpu.make_async_copy(lg_v, lg_h, store.at[0]).start()
    pltpu.make_async_copy(rg_v, rg_h, store.at[1]).start()
    adapted = ADAPTER_SCALE * dot(low, right, TN)

    pair_copy(y, q).wait_recv()
    total = part[f].astype(F32) + pair[y].astype(F32) + adapted
    base[:, 0:feat] = total

    @pl.loop(1, NY)
    def _(j):
        yy = lax.rem(y - j + NY, NY)
        sum_copy(y, yy).wait_recv()
        base[:, 0:feat] += fromy[yy].astype(F32)

    outrows[...] = base[:, 0:feat].astype(BF16).reshape(C, CAP, feat)

    @pl.loop(1, C)
    def _(i):
        other = lax.rem(c + i, C)
        ret_copy(other, c).start()

    ret[c] = outrows[c]

    @pl.loop(1, C)
    def _(i):
        other = lax.rem(c + i, C)
        tok_copy(other, c).wait_send()
        grad_copy(other, c).wait_send()

    @pl.loop(0, C)
    def _(b):
        @pl.loop(1, NY)
        def _(j):
            y_copy(b, lax.rem(y + j, NY), y).wait_send()

        @pl.loop(0, NY)
        def _(yy):
            k_copy(yy, b, q).wait_send()

    @pl.loop(1, F)
    def _(j):
        other = lax.rem(f + j, F)
        rank_copy(rank_b, bS, bR, other, f).wait_send()
        rank_copy(rank_l, lS, lR, other, f).wait_send()

    @pl.loop(0, NY)
    def _(yy):
        pair_copy(yy, 1 - q).wait_send()

    @pl.loop(1, NY)
    def _(j):
        sum_copy(lax.rem(y + j, NY), y).wait_send()

    wfull = wd[...]
    whigh = wfull.astype(BF16)
    wlow = (wfull - whigh.astype(F32)).astype(BF16)

    @pl.loop(1, C)
    def _(i):
        b = lax.rem(c - i + C, C)
        ret_copy(b, b).wait_recv()

    back_rows = ret[...].reshape(R, feat)
    out_v[...] = (dot(back_rows, whigh, TN) + dot(back_rows, wlow, TN)).astype(BF16)
    pltpu.make_async_copy(out_v, out_h, store.at[2]).start()

    @pl.loop(1, C)
    def _(i):
        other = lax.rem(c + i, C)
        ret_copy(other, c).wait_send()

    pltpu.make_async_copy(lg_v, lg_h, store.at[0]).wait()
    pltpu.make_async_copy(rg_v, rg_h, store.at[1]).wait()
    pltpu.make_async_copy(out_v, out_h, store.at[2]).wait()


def on_device(
    tokens,
    cotangent,
    expert_indices,
    routing_weights,
    gate_up_weight_blocks,
    gate_up_block_scales,
    down_weight_blocks,
    down_block_scales,
    adapter_down_matrix,
    adapter_up_matrix,
):
    C = lax.axis_size("ctx")
    F = lax.axis_size("exp")
    NY = F // 2
    T, feat = tokens.shape
    top = expert_indices.shape[1]
    _, H, width = down_weight_blocks.shape
    rank = adapter_up_matrix.shape[1]
    R = C * CAP
    NB = width // BLOCK
    hpad = -(-H // 128) * 128
    bpad = -(-NB // 128) * 128
    dma = pltpu.SemaphoreType.DMA
    scratch = [
        pltpu.VMEM((feat, T), BF16),
        pltpu.VMEM((feat, T), BF16),
        pltpu.VMEM((top, T), jnp.int32),
        pltpu.VMEM((top, T), F32),
        pltpu.VMEM((3, H, width), BF16),
        pltpu.VMEM((NB, 2, H), F32),
        pltpu.VMEM((NB, 1, H), F32),
        pltpu.VMEM((rank, H), BF16),
        pltpu.VMEM((rank, feat), BF16),
        pltpu.VMEM((bpad, hpad), F32),
        pltpu.VMEM((3, H, bpad), BF16),
        pltpu.VMEM((bpad, width), BF16),
        pltpu.VMEM((C, CAP, feat), BF16),
        pltpu.VMEM((C, CAP, feat), BF16),
        pltpu.VMEM((F, C, CAP, feat), BF16),
        pltpu.VMEM((C, CAP, feat), BF16),
        pltpu.VMEM((R, width), BF16),
        pltpu.VMEM((R, T), F32),
        pltpu.VMEM((R, width), F32),
        pltpu.VMEM((F, R, feat), BF16),
        pltpu.VMEM((NY, R, feat), BF16),
        pltpu.VMEM((NY, R, feat), BF16),
        pltpu.VMEM((NY, R, feat), BF16),
        pltpu.VMEM((F, rank, R), BF16),
        pltpu.VMEM((F, rank, R), BF16),
        pltpu.VMEM((C, CAP, feat), BF16),
        pltpu.VMEM((C, CAP, feat), BF16),
        pltpu.VMEM((feat, T), BF16),
        pltpu.VMEM((rank, H), F32),
        pltpu.VMEM((rank, feat), F32),
        dma((11,)), dma((3,)),
        dma((C,)), dma((C,)), dma((C,)), dma((C,)), dma((C,)), dma((C,)),
        dma((NY, C)), dma((NY, C)), dma((NY, C)), dma((NY, C)),
        dma((F,)), dma((F,)), dma((F,)), dma((F,)),
        dma((NY,)), dma((NY,)), dma((NY,)), dma((NY,)),
    ]
    any_space = pl.BlockSpec(memory_space=pl.ANY)
    out_t, left_t, right = pl.pallas_call(
        functools.partial(block_kernel, C, F),
        out_shape=(
            jax.ShapeDtypeStruct((feat, T), BF16),
            jax.ShapeDtypeStruct((rank, H), F32),
            jax.ShapeDtypeStruct((rank, feat), F32),
        ),
        in_specs=[any_space] * 10,
        out_specs=(any_space,) * 3,
        scratch_shapes=scratch,
        compiler_params=pltpu.CompilerParams(
            collective_id=0, has_side_effects=True, vmem_limit_bytes=52 * 2**20
        ),
    )(
        tokens.T,
        cotangent.T,
        expert_indices.T,
        routing_weights.T,
        gate_up_weight_blocks[0],
        jnp.transpose(gate_up_block_scales[0], (2, 0, 1)),
        down_weight_blocks[0],
        jnp.transpose(down_block_scales, (2, 0, 1)),
        adapter_down_matrix[0].T,
        adapter_up_matrix[0],
    )
    return out_t.T, left_t.T[None], right[None]


def solution(mesh):
    placed = (
        P("ctx", "exp"),
        P("ctx", "exp"),
        P("ctx", None),
        P("ctx", None),
        P("ctx", None, "exp", None),
        P("ctx", None, "exp", None),
        P("ctx", "exp", None),
        P("ctx", "exp", None),
        P("ctx", "exp", None),
        P("ctx", None, "exp"),
    )
    return jax.shard_map(
        on_device,
        mesh=mesh,
        in_specs=placed,
        out_specs=(P("ctx", "exp"), P("ctx", "exp", None), P("ctx", None, "exp")),
        check_vma=False,
    )
```

```python
import functools

import jax
import jax.numpy as jnp
from jax import lax
from jax.experimental import pallas as pl
from jax.experimental.pallas import tpu as pltpu
from jax.sharding import PartitionSpec as P

CAP = 16
BLOCK = 32
ADAPTER_SCALE = 0.5
GLU_ALPHA = 1.702
CLAMP_LIMIT = 7.0

F32 = jnp.float32
BF16 = jnp.bfloat16
NN = (((1,), (0,)), ((), ()))
NT = (((1,), (1,)), ((), ()))
TN = (((0,), (0,)), ((), ()))


def dot(a, b, dims):
    return lax.dot_general(a, b, dims, preferred_element_type=F32)


def unit_rows(hidden):
    for rows in (240, 144, 128, 80, 48, 16):
        if hidden % rows == 0:
            return rows
    return hidden


def block_kernel(
    C, F,
    tok_h, cot_h, idx_h, rw_h, gu_h, gus_h, dn_h, dns_h, adl_h, adu_h,
    ret, wd, lg_v, rg_v,
    tok, cot, idx, rw, raw, gus, dns, adl, adu,
    spad, ssc, expand, rows, grows, xin, gin, xfull,
    base, part, pair, tosend, fromy, rank_b, rank_l, outrows, adapt,
    load, tS, tR, gS, gR, rS, rR, yS, yR, kS, kR, bS, bR, lS, lR, pS, pR, qS, qR,
):
    NY = F // 2
    H, width = raw.shape[1], raw.shape[2]
    feat = tok.shape[0]
    T = tok.shape[1]
    R = C * CAP
    NB = width // BLOCK
    c = lax.axis_index("ctx")
    f = lax.axis_index("exp")
    y = f // 2
    q = f % 2
    mate = f + 1 - 2 * q

    def at_ctx(other):
        return dict(device_id=(other, f), device_id_type=pl.DeviceIdType.MESH)

    def at_exp(other):
        return dict(device_id=(c, other), device_id_type=pl.DeviceIdType.MESH)

    barrier = pltpu.get_barrier_semaphore()

    @pl.loop(1, C)
    def _(i):
        pl.semaphore_signal(barrier, inc=1, **at_ctx(lax.rem(c + i, C)))

    @pl.loop(1, F)
    def _(i):
        pl.semaphore_signal(barrier, inc=1, **at_exp(lax.rem(f + i, F)))

    loads = [
        pltpu.make_async_copy(idx_h, idx, load.at[0]),
        pltpu.make_async_copy(tok_h, tok, load.at[1]),
        pltpu.make_async_copy(rw_h, rw, load.at[2]),
        pltpu.make_async_copy(cot_h, cot, load.at[3]),
        pltpu.make_async_copy(gus_h, gus, load.at[4]),
        pltpu.make_async_copy(dns_h, dns, load.at[5]),
        pltpu.make_async_copy(gu_h.at[0], raw.at[0], load.at[6]),
        pltpu.make_async_copy(gu_h.at[1], raw.at[1], load.at[7]),
        pltpu.make_async_copy(dn_h, raw.at[2], load.at[8]),
        pltpu.make_async_copy(adl_h, adl, load.at[9]),
        pltpu.make_async_copy(adu_h, adu, load.at[10]),
    ]
    for copy in loads:
        copy.start()

    loads[0].wait()
    slot = lax.broadcasted_iota(jnp.int32, (R, T), 0)
    expert = lax.shift_right_logical(slot, 4)
    number = lax.bitwise_and(slot, 15).astype(F32)
    named = idx[0:1, :] == expert
    for k in range(1, idx.shape[0]):
        named = jnp.logical_or(named, idx[k:k + 1, :] == expert)
    earlier = (
        lax.broadcasted_iota(jnp.int32, (T, T), 0) < lax.broadcasted_iota(jnp.int32, (T, T), 1)
    ).astype(F32).astype(BF16)
    position = dot(named.astype(F32).astype(BF16), earlier, NN)
    hit = jnp.logical_and(named, position == number)
    pick = hit.astype(F32).astype(BF16)
    loads[1].wait()
    rows[...] = dot(pick, tok[...], NT).astype(BF16).reshape(C, CAP, feat)

    pl.semaphore_wait(barrier, C - 1 + F - 1)

    def send_rows(src, dst, ss, rs, other, **where):
        return pltpu.make_async_remote_copy(
            src_ref=src, dst_ref=dst, send_sem=ss, recv_sem=rs, **where
        )

    def tok_copy(other, came):
        return send_rows(rows.at[other], xin.at[f, came], tS.at[other], tR.at[came], other, **at_ctx(other))

    def grad_copy(other, came):
        return send_rows(grows.at[other], gin.at[came], gS.at[other], gR.at[came], other, **at_ctx(other))

    def ret_copy(other, came):
        return send_rows(outrows.at[other], ret.at[came], rS.at[other], rR.at[came], other, **at_ctx(other))

    def y_copy(b, yy, came):
        return send_rows(
            xin.at[2 * came + q, b], xin.at[2 * came + q, b], yS.at[yy, b], yR.at[came, b], 0,
            **at_exp(2 * yy + q),
        )

    def k_copy(yy, b, core):
        return send_rows(
            xin.at[2 * yy + core, b], xin.at[2 * yy + core, b], kS.at[yy, b], kR.at[yy, b], 0,
            **at_exp(mate),
        )

    @pl.loop(1, C)
    def _(i):
        other = lax.rem(c + i, C)
        tok_copy(other, c).start()

    xin[f, c] = rows[c]

    loads[2].wait()
    weight = jnp.zeros((R, T), F32)
    for k in range(idx.shape[0]):
        weight = weight + jnp.where(idx[k:k + 1, :] == expert, rw[k:k + 1, :], 0.0)
    weight = jnp.where(hit, weight, 0.0)
    wd[...] = weight
    loads[3].wait()
    picked = dot(pick, cot[...], NT) * jnp.sum(weight, axis=1, keepdims=True)
    grows[...] = picked.astype(BF16).reshape(C, CAP, feat)

    expand[...] = (
        lax.shift_right_logical(lax.broadcasted_iota(jnp.int32, expand.shape, 1), 5)
        == lax.broadcasted_iota(jnp.int32, expand.shape, 0)
    ).astype(F32).astype(BF16)
    spad[...] = jnp.zeros_like(spad)
    loads[4].wait()
    loads[5].wait()
    for m in range(3):
        if m < 2:
            spad[0:NB, 0:H] = gus[:, m, :]
        else:
            spad[0:NB, 0:H] = dns[:, 0, :]
        ssc[m] = jnp.transpose(spad[...]).astype(BF16)[0:H]
    unit = unit_rows(H)
    per = H // unit
    lanes = 256

    def dequant(u):
        m = u // per
        at = pl.ds(pl.multiple_of(lax.rem(u, per) * unit, unit), unit) if per > 1 else slice(None)
        scale = ssc[m, at, :]
        for lo in range(0, width, lanes):
            hi = min(lo + lanes, width)
            spread = dot(scale, expand[:, lo:hi], NN).astype(BF16)
            raw[m, at, lo:hi] = raw[m, at, lo:hi] * spread

    def forward(i):
        b = lax.rem(c - i + C, C)

        @pl.when(i > 0)
        def _():
            tok_copy(b, b).wait_recv()

        @pl.loop(1, NY)
        def _(j):
            y_copy(b, lax.rem(y + j, NY), y).start()

        k_copy(y, b, q).start()

    def y_forward(i):
        yy = lax.rem(y - 1 - i // C + NY, NY)
        b = lax.rem(c - lax.rem(i, C) + C, C)
        y_copy(b, y, yy).wait_recv()
        k_copy(yy, b, q).start()

    units = 3 * per
    events = NY * C

    @pl.loop(0, max(events, units))
    def _(s):
        for m in range(3):
            @pl.when(s == m * per)
            def _():
                loads[6 + m].wait()

        @pl.when(s < units)
        def _():
            dequant(s)

        @pl.when(s < C)
        def _():
            forward(s)

        @pl.when(jnp.logical_and(s >= C, s < events))
        def _():
            y_forward(s - C)

    @pl.loop(1, C)
    def _(i):
        other = lax.rem(c + i, C)
        grad_copy(other, c).start()

    gin[c] = grows[c]

    @pl.loop(0, NY)
    def _(yy):
        @pl.loop(0, C)
        def _(b):
            k_copy(yy, b, 1 - q).wait_recv()

    def rank_copy(buf, ss, rs, other, came):
        return send_rows(buf.at[came], buf.at[came], ss.at[other], rs.at[came], other, **at_exp(other))

    for g in range(F):
        xfull[:, g * feat:(g + 1) * feat] = xin[g].reshape(R, feat)
    x = xfull[...]
    gate = jnp.minimum(dot(x, raw[0], NT), CLAMP_LIMIT)
    up = jnp.clip(dot(x, raw[1], NT), -CLAMP_LIMIT, CLAMP_LIMIT)
    activated = ((up + 1.0) * gate / (1.0 + jnp.exp(-GLU_ALPHA * gate))).astype(BF16)

    loads[9].wait()
    loads[10].wait()
    rank_l[f] = dot(adl[...], activated, NT).astype(BF16)

    @pl.loop(1, F)
    def _(j):
        rank_copy(rank_l, lS, lR, lax.rem(f + j, F), f).start()

    base[...] = dot(activated, raw[2], NN)
    for g in range(F):
        part[g] = base[:, g * feat:(g + 1) * feat].astype(BF16).reshape(C, CAP, feat)

    NG = 4 if C % 4 == 0 else 1
    GB = C // NG
    mine = c // GB

    def span(g):
        return pl.ds(g * GB, GB)

    def pair_copy(yy, g, core):
        return send_rows(
            part.at[2 * yy + core, span(g)], pair.at[yy, span(g)], pS.at[yy, g], pR.at[yy, g], 0,
            **at_exp(mate),
        )

    def sum_copy(yy, g, came):
        return send_rows(
            tosend.at[yy, span(g)], fromy.at[came, span(g)], qS.at[yy, g], qR.at[came, g], 0,
            **at_exp(2 * yy + q),
        )

    @pl.loop(1, NY + 1)
    def _(j):
        @pl.loop(1, NG + 1)
        def _(n):
            pair_copy(lax.rem(y + j, NY), lax.rem(mine + n, NG), 1 - q).start()

    @pl.loop(1, NG + 1)
    def _(n):
        g = lax.rem(mine + n, NG)

        @pl.loop(1, NY)
        def _(j):
            yy = lax.rem(y + j, NY)
            pair_copy(yy, g, q).wait_recv()
            tosend[yy, span(g)] = (
                part[2 * yy + q, span(g)].astype(F32) + pair[yy, span(g)].astype(F32)
            ).astype(BF16)
            sum_copy(yy, g, y).start()

    @pl.loop(1, F)
    def _(j):
        other = lax.rem(f - j + F, F)
        rank_copy(rank_l, lS, lR, other, other).wait_recv()

    low = rank_l[0].astype(F32)
    for g in range(1, F):
        low = low + rank_l[g].astype(F32)
    low = low.astype(BF16)
    adapt[...] = (ADAPTER_SCALE * dot(low, adu[...], TN)).reshape(C, CAP, feat)

    @pl.loop(1, NG + 1)
    def _(n):
        g = lax.rem(mine + n, NG)
        pair_copy(y, g, q).wait_recv()
        adapt[span(g)] += part[f, span(g)].astype(F32) + pair[y, span(g)].astype(F32)

        @pl.loop(1, NY)
        def _(j):
            yy = lax.rem(y - j + NY, NY)
            sum_copy(y, g, yy).wait_recv()
            adapt[span(g)] += fromy[yy, span(g)].astype(F32)

        outrows[span(g)] = adapt[span(g)].astype(BF16)

        @pl.loop(0, GB)
        def _(i):
            other = g * GB + i

            @pl.when(other != c)
            def _():
                ret_copy(other, c).start()

    ret[c] = outrows[c]

    @pl.loop(1, C)
    def _(i):
        b = lax.rem(c - i + C, C)
        grad_copy(b, b).wait_recv()

    grads = gin[...].reshape(R, feat)
    rank_b[f] = dot(adu[...], grads, NT).astype(BF16)

    @pl.loop(1, F)
    def _(j):
        rank_copy(rank_b, bS, bR, lax.rem(f + j, F), f).start()

    @pl.loop(1, F)
    def _(j):
        other = lax.rem(f - j + F, F)
        rank_copy(rank_b, bS, bR, other, other).wait_recv()

    back = rank_b[0].astype(F32)
    for g in range(1, F):
        back = back + rank_b[g].astype(F32)
    back = (ADAPTER_SCALE * back).astype(BF16)
    lg_v[...] = dot(back, activated, NN)
    rg_v[...] = ADAPTER_SCALE * dot(low, grads, NN)

    @pl.loop(1, C)
    def _(i):
        other = lax.rem(c + i, C)
        tok_copy(other, c).wait_send()
        grad_copy(other, c).wait_send()

    @pl.loop(0, C)
    def _(b):
        @pl.loop(1, NY)
        def _(j):
            y_copy(b, lax.rem(y + j, NY), y).wait_send()

        @pl.loop(0, NY)
        def _(yy):
            k_copy(yy, b, q).wait_send()

    @pl.loop(1, F)
    def _(j):
        other = lax.rem(f + j, F)
        rank_copy(rank_b, bS, bR, other, f).wait_send()
        rank_copy(rank_l, lS, lR, other, f).wait_send()

    @pl.loop(0, NG)
    def _(g):
        @pl.loop(0, NY)
        def _(yy):
            pair_copy(yy, g, 1 - q).wait_send()

        @pl.loop(1, NY)
        def _(j):
            sum_copy(lax.rem(y + j, NY), g, y).wait_send()

    @pl.loop(1, C)
    def _(i):
        b = lax.rem(c - i + C, C)
        ret_copy(b, b).wait_recv()

    @pl.loop(1, C)
    def _(i):
        other = lax.rem(c + i, C)
        ret_copy(other, c).wait_send()


def combine_kernel(ret, wd, lg, rg, out_h, lg_h, rg_h, out, sems):
    C, _, feat = ret.shape
    left = pltpu.make_async_copy(lg, lg_h, sems.at[0])
    right = pltpu.make_async_copy(rg, rg_h, sems.at[1])
    left.start()
    right.start()
    weight = wd[...]
    high = weight.astype(BF16)
    rest = (weight - high.astype(F32)).astype(BF16)
    rows = ret[...].reshape(C * CAP, feat)
    out[...] = (dot(rows, high, TN) + dot(rows, rest, TN)).astype(BF16)
    result = pltpu.make_async_copy(out, out_h, sems.at[2])
    result.start()
    left.wait()
    right.wait()
    result.wait()


def on_device(
    tokens,
    cotangent,
    expert_indices,
    routing_weights,
    gate_up_weight_blocks,
    gate_up_block_scales,
    down_weight_blocks,
    down_block_scales,
    adapter_down_matrix,
    adapter_up_matrix,
):
    C = lax.axis_size("ctx")
    F = lax.axis_size("exp")
    NY = F // 2
    T, feat = tokens.shape
    top = expert_indices.shape[1]
    _, H, width = down_weight_blocks.shape
    rank = adapter_up_matrix.shape[1]
    R = C * CAP
    NB = width // BLOCK
    hpad = -(-H // 128) * 128
    bpad = -(-NB // 128) * 128
    NG = 4 if C % 4 == 0 else 1
    dma = pltpu.SemaphoreType.DMA
    scratch = [
        pltpu.VMEM((feat, T), BF16),
        pltpu.VMEM((feat, T), BF16),
        pltpu.VMEM((top, T), jnp.int32),
        pltpu.VMEM((top, T), F32),
        pltpu.VMEM((3, H, width), BF16),
        pltpu.VMEM((NB, 2, H), F32),
        pltpu.VMEM((NB, 1, H), F32),
        pltpu.VMEM((rank, H), BF16),
        pltpu.VMEM((rank, feat), BF16),
        pltpu.VMEM((bpad, hpad), F32),
        pltpu.VMEM((3, H, bpad), BF16),
        pltpu.VMEM((bpad, width), BF16),
        pltpu.VMEM((C, CAP, feat), BF16),
        pltpu.VMEM((C, CAP, feat), BF16),
        pltpu.VMEM((F, C, CAP, feat), BF16),
        pltpu.VMEM((C, CAP, feat), BF16),
        pltpu.VMEM((R, width), BF16),
        pltpu.VMEM((R, width), F32),
        pltpu.VMEM((F, C, CAP, feat), BF16),
        pltpu.VMEM((NY, C, CAP, feat), BF16),
        pltpu.VMEM((NY, C, CAP, feat), BF16),
        pltpu.VMEM((NY, C, CAP, feat), BF16),
        pltpu.VMEM((F, rank, R), BF16),
        pltpu.VMEM((F, rank, R), BF16),
        pltpu.VMEM((C, CAP, feat), BF16),
        pltpu.VMEM((C, CAP, feat), F32),
        dma((11,)),
        dma((C,)), dma((C,)), dma((C,)), dma((C,)), dma((C,)), dma((C,)),
        dma((NY, C)), dma((NY, C)), dma((NY, C)), dma((NY, C)),
        dma((F,)), dma((F,)), dma((F,)), dma((F,)),
        dma((NY, NG)), dma((NY, NG)), dma((NY, NG)), dma((NY, NG)),
    ]
    in_hbm = pl.BlockSpec(memory_space=pltpu.HBM)
    in_vmem = pl.BlockSpec(memory_space=pltpu.VMEM)
    mid = pl.pallas_call(
        functools.partial(block_kernel, C, F),
        out_shape=(
            jax.ShapeDtypeStruct((C, CAP, feat), BF16),
            jax.ShapeDtypeStruct((R, T), F32),
            jax.ShapeDtypeStruct((rank, H), F32),
            jax.ShapeDtypeStruct((rank, feat), F32),
        ),
        in_specs=[in_hbm] * 10,
        out_specs=(in_vmem,) * 4,
        scratch_shapes=scratch,
        compiler_params=pltpu.CompilerParams(
            collective_id=0, has_side_effects=True, vmem_limit_bytes=52 * 2**20
        ),
    )(
        *(
            pltpu.with_memory_space_constraint(x, pltpu.HBM)
            for x in (
                tokens.T,
                cotangent.T,
                expert_indices.T,
                routing_weights.T,
                gate_up_weight_blocks[0],
                jnp.transpose(gate_up_block_scales[0], (2, 0, 1)),
                down_weight_blocks[0],
                jnp.transpose(down_block_scales, (2, 0, 1)),
                adapter_down_matrix[0].T,
                adapter_up_matrix[0],
            )
        )
    )
    out_t, left_t, right = pl.pallas_call(
        combine_kernel,
        out_shape=(
            jax.ShapeDtypeStruct((feat, T), BF16),
            jax.ShapeDtypeStruct((rank, H), F32),
            jax.ShapeDtypeStruct((rank, feat), F32),
        ),
        in_specs=[in_vmem] * 4,
        out_specs=(in_hbm,) * 3,
        scratch_shapes=[pltpu.VMEM((feat, T), BF16), dma((3,))],
        compiler_params=pltpu.CompilerParams(vmem_limit_bytes=16 * 2**20),
    )(*mid)
    return out_t.T, left_t.T[None], right[None]


def solution(mesh):
    placed = (
        P("ctx", "exp"),
        P("ctx", "exp"),
        P("ctx", None),
        P("ctx", None),
        P("ctx", None, "exp", None),
        P("ctx", None, "exp", None),
        P("ctx", "exp", None),
        P("ctx", "exp", None),
        P("ctx", "exp", None),
        P("ctx", None, "exp"),
    )
    return jax.shard_map(
        on_device,
        mesh=mesh,
        in_specs=placed,
        out_specs=(P("ctx", "exp"), P("ctx", "exp", None), P("ctx", None, "exp")),
        check_vma=False,
    )
```

```python
import functools

import jax
import jax.numpy as jnp
from jax import lax
from jax.experimental import pallas as pl
from jax.experimental.pallas import tpu as pltpu
from jax.sharding import PartitionSpec as P

CAP = 16
BLOCK = 32
ADAPTER_SCALE = 0.5
GLU_ALPHA = 1.702
CLAMP_LIMIT = 7.0

F32 = jnp.float32
BF16 = jnp.bfloat16
NN = (((1,), (0,)), ((), ()))
NT = (((1,), (1,)), ((), ()))
TN = (((0,), (0,)), ((), ()))


def dot(a, b, dims):
    return lax.dot_general(a, b, dims, preferred_element_type=F32)


def unit_rows(hidden):
    for rows in (144, 128, 80, 48, 16):
        if hidden % rows == 0:
            return rows
    return hidden


def block_kernel(
    C, F,
    tok_h, cot_h, idx_h, rw_h, gu_h, gus_h, dn_h, dns_h, adl_h, adu_h,
    ret, wd, lg_v, rg_v,
    tok, cot, idx, rw, raw, gus, dns, adl, adu,
    spad, ssc, expand, rows, grows, xin, gin, xh, acc,
    base, part, pair, tosend, fromy, rank_b, rank_l, outrows, adapt,
    load, tS, tR, gS, gR, rS, rR, yS, yR, kS, kR, bS, bR, lS, lR, pS, pR, qS, qR,
):
    NY = F // 2
    H, width = raw.shape[1], raw.shape[2]
    feat = tok.shape[0]
    T = tok.shape[1]
    R = C * CAP
    NB = width // BLOCK
    c = lax.axis_index("ctx")
    f = lax.axis_index("exp")
    y = f // 2
    q = f % 2
    mate = f + 1 - 2 * q

    def at_ctx(other):
        return dict(device_id=(other, f), device_id_type=pl.DeviceIdType.MESH)

    def at_exp(other):
        return dict(device_id=(c, other), device_id_type=pl.DeviceIdType.MESH)

    def paired(me, i, n):
        if n & (n - 1):
            return lax.rem(me + i, n)
        other, bit = 0, 1
        while bit < n:
            other = other + lax.rem(me // bit + i // bit, 2) * bit
            bit *= 2
        return other

    def from_pair(me, i, n):
        if n & (n - 1):
            return lax.rem(me - i + n, n)
        return paired(me, i, n)

    barrier = pltpu.get_barrier_semaphore()

    @pl.loop(1, C)
    def _(i):
        pl.semaphore_signal(barrier, inc=1, **at_ctx(lax.rem(c + i, C)))

    @pl.loop(1, F)
    def _(i):
        pl.semaphore_signal(barrier, inc=1, **at_exp(lax.rem(f + i, F)))

    loads = [
        pltpu.make_async_copy(idx_h, idx, load.at[0]),
        pltpu.make_async_copy(tok_h, tok, load.at[1]),
        pltpu.make_async_copy(rw_h, rw, load.at[2]),
        pltpu.make_async_copy(cot_h, cot, load.at[3]),
        pltpu.make_async_copy(gus_h, gus, load.at[4]),
        pltpu.make_async_copy(dns_h, dns, load.at[5]),
        pltpu.make_async_copy(gu_h.at[0], raw.at[0], load.at[6]),
        pltpu.make_async_copy(gu_h.at[1], raw.at[1], load.at[7]),
        pltpu.make_async_copy(dn_h, raw.at[2], load.at[8]),
        pltpu.make_async_copy(adl_h, adl, load.at[9]),
        pltpu.make_async_copy(adu_h, adu, load.at[10]),
    ]
    for copy in loads:
        copy.start()

    expand[...] = (
        lax.shift_right_logical(lax.broadcasted_iota(jnp.int32, expand.shape, 1), 5)
        == lax.broadcasted_iota(jnp.int32, expand.shape, 0)
    ).astype(F32).astype(BF16)
    spad[...] = jnp.zeros_like(spad)
    xh[...] = jnp.zeros_like(xh)

    loads[0].wait()
    slot = lax.broadcasted_iota(jnp.int32, (R, T), 0)
    expert = lax.shift_right_logical(slot, 4)
    number = lax.bitwise_and(slot, 15).astype(F32)
    named = idx[0:1, :] == expert
    for k in range(1, idx.shape[0]):
        named = jnp.logical_or(named, idx[k:k + 1, :] == expert)
    earlier = (
        lax.broadcasted_iota(jnp.int32, (T, T), 0) < lax.broadcasted_iota(jnp.int32, (T, T), 1)
    ).astype(F32).astype(BF16)
    position = dot(named.astype(F32).astype(BF16), earlier, NN)
    hit = jnp.logical_and(named, position == number)
    pick = hit.astype(F32).astype(BF16)
    loads[1].wait()
    rows[...] = dot(pick, tok[...], NT).astype(BF16).reshape(C, CAP, feat)

    pl.semaphore_wait(barrier, C - 1 + F - 1)

    def send_rows(src, dst, ss, rs, other, **where):
        return pltpu.make_async_remote_copy(
            src_ref=src, dst_ref=dst, send_sem=ss, recv_sem=rs, **where
        )

    def tok_copy(other, came):
        return send_rows(rows.at[other], xin.at[f, came], tS.at[other], tR.at[came], other, **at_ctx(other))

    def grad_copy(other, came):
        return send_rows(grows.at[other], gin.at[came], gS.at[other], gR.at[came], other, **at_ctx(other))

    def ret_copy(other, came):
        return send_rows(outrows.at[other], ret.at[came], rS.at[other], rR.at[came], other, **at_ctx(other))

    def y_copy(b, yy, came):
        return send_rows(
            xin.at[2 * came + q, b], xin.at[2 * came + q, b], yS.at[yy, b], yR.at[came, b], 0,
            **at_exp(2 * yy + q),
        )

    def k_copy(yy, b, core):
        return send_rows(
            xin.at[2 * yy + core, b], xin.at[2 * yy + core, b], kS.at[yy, b], kR.at[yy, b], 0,
            **at_exp(mate),
        )

    @pl.loop(1, C)
    def _(i):
        tok_copy(paired(c, C - i, C), c).start()

    xin[f, c] = rows[c]

    def forward(i):
        b = from_pair(c, i, C)

        if not isinstance(i, int):
            tok_copy(b, b).wait_recv()

        @pl.loop(1, NY)
        def _(j):
            y_copy(b, lax.rem(y + j, NY), y).start()

        k_copy(y, b, q).start()
    forward(0)

    loads[4].wait()
    loads[5].wait()
    for m in range(3):
        if m < 2:
            spad[0:NB, 0:H] = gus[:, m, :]
        else:
            spad[0:NB, 0:H] = dns[:, 0, :]
        ssc[m] = jnp.transpose(spad[...]).astype(BF16)[0:H]
    unit = unit_rows(H)
    per = H // unit
    lanes = 256

    def dequant(u):
        m = u // per
        at = pl.ds(pl.multiple_of(lax.rem(u, per) * unit, unit), unit) if per > 1 else slice(None)
        scale = ssc[m, at, :]
        for lo in range(0, width, lanes):
            hi = min(lo + lanes, width)
            spread = dot(scale, expand[:, lo:hi], NN).astype(BF16)
            raw[m, at, lo:hi] = raw[m, at, lo:hi] * spread

    def y_forward(i):
        yy = lax.rem(y - 1 - i // C + NY, NY)
        b = from_pair(c, lax.rem(i, C), C)
        y_copy(b, y, yy).wait_recv()
        k_copy(yy, b, q).start()

    units = 3 * per
    events = NY * C

    @pl.loop(0, max(events, units))
    def _(s):
        for m in range(3):
            @pl.when(s == m * per)
            def _():
                loads[6 + m].wait()

        @pl.when(s < units)
        def _():
            dequant(s)

        @pl.when(jnp.logical_and(s > 0, s < C))
        def _():
            forward(s)

        @pl.when(jnp.logical_and(s >= C, s < events))
        def _():
            y_forward(s - C)

    loads[2].wait()
    weight = jnp.zeros((R, T), F32)
    for k in range(idx.shape[0]):
        weight = weight + jnp.where(idx[k:k + 1, :] == expert, rw[k:k + 1, :], 0.0)
    weight = jnp.where(hit, weight, 0.0)
    wd[...] = weight
    loads[3].wait()
    picked = dot(pick, cot[...], NT) * jnp.sum(weight, axis=1, keepdims=True)
    grows[...] = picked.astype(BF16).reshape(C, CAP, feat)

    @pl.loop(1, C)
    def _(i):
        grad_copy(paired(c, C - i, C), c).start()

    gin[c] = grows[c]

    def rank_copy(buf, ss, rs, other, came):
        return send_rows(buf.at[came], buf.at[came], ss.at[other], rs.at[came], other, **at_exp(other))

    def window(yy):
        lo = 2 * feat * yy // 128 * 128
        return lo, min(width, -(-2 * feat * (yy + 1) // 128) * 128)

    def arrived(yy):
        @pl.loop(0, C)
        def _(b):
            k_copy(yy, b, 1 - q).wait_recv()

    def project(yy):
        lo, hi = window(yy)
        at = 2 * feat * yy - lo
        for core in range(2):
            xh[yy, :, at:at + feat] = xin[2 * yy + core].reshape(R, feat)
            at += feat
        x = xh[yy, :, 0:hi - lo]
        return dot(x, raw[0, :, lo:hi], NT), dot(x, raw[1, :, lo:hi], NT)

    arrived(y)
    for yy in range(NY):
        @pl.when(y == yy)
        def _():
            gate_part, up_part = project(yy)
            acc[0] = gate_part
            acc[1] = up_part

    for yy in range(NY):
        @pl.when(y != yy)
        def _():
            arrived(yy)
            gate_part, up_part = project(yy)
            acc[0] += gate_part
            acc[1] += up_part

    gate = jnp.minimum(acc[0], CLAMP_LIMIT)
    up = jnp.clip(acc[1], -CLAMP_LIMIT, CLAMP_LIMIT)
    activated = ((up + 1.0) * gate / (1.0 + jnp.exp(-GLU_ALPHA * gate))).astype(BF16)

    loads[9].wait()
    loads[10].wait()
    rank_l[f] = dot(adl[...], activated, NT).astype(BF16)

    @pl.loop(1, F)
    def _(j):
        rank_copy(rank_l, lS, lR, lax.rem(f + j, F), f).start()

    def columns(yy):
        lo, hi = window(yy)
        base[:, 0:hi - lo] = dot(activated, raw[2, :, lo:hi], NN)
        at = 2 * feat * yy - lo
        for core in range(2):
            part[2 * yy + core] = base[:, at:at + feat].astype(BF16).reshape(C, CAP, feat)
            at += feat

    NG = 4 if C % 4 == 0 else 1
    GB = C // NG
    mine = c // GB

    def span(g):
        return pl.ds(g * GB, GB)

    def pair_copy(yy, g, core):
        return send_rows(
            part.at[2 * yy + core, span(g)], pair.at[yy, span(g)], pS.at[yy, g], pR.at[yy, g], 0,
            **at_exp(mate),
        )

    def sum_copy(yy, g, came):
        return send_rows(
            tosend.at[yy, span(g)], fromy.at[came, span(g)], qS.at[yy, g], qR.at[came, g], 0,
            **at_exp(2 * yy + q),
        )

    def to_mate(yy):
        @pl.loop(1, NG + 1)
        def _(n):
            pair_copy(yy, paired(mine, NG - n, NG), 1 - q).start()

    for yy in range(NY):
        @pl.when(y != yy)
        def _():
            columns(yy)
            to_mate(yy)

    @pl.loop(1, NG + 1)
    def _(n):
        g = paired(mine, NG - n, NG)

        @pl.loop(1, NY)
        def _(j):
            yy = lax.rem(y + j, NY)
            pair_copy(yy, g, q).wait_recv()
            tosend[yy, span(g)] = (
                part[2 * yy + q, span(g)].astype(F32) + pair[yy, span(g)].astype(F32)
            ).astype(BF16)
            sum_copy(yy, g, y).start()

    for yy in range(NY):
        @pl.when(y == yy)
        def _():
            columns(yy)
            to_mate(yy)

    @pl.loop(1, F)
    def _(j):
        other = lax.rem(f - j + F, F)
        rank_copy(rank_l, lS, lR, other, other).wait_recv()

    low = rank_l[0].astype(F32)
    for g in range(1, F):
        low = low + rank_l[g].astype(F32)
    low = low.astype(BF16)
    adapt[...] = (ADAPTER_SCALE * dot(low, adu[...], TN)).reshape(C, CAP, feat)

    @pl.loop(1, NG + 1)
    def _(n):
        g = paired(mine, NG - n, NG)
        pair_copy(y, g, q).wait_recv()
        adapt[span(g)] += part[f, span(g)].astype(F32) + pair[y, span(g)].astype(F32)

        @pl.loop(1, NY)
        def _(j):
            yy = lax.rem(y - j + NY, NY)
            sum_copy(y, g, yy).wait_recv()
            adapt[span(g)] += fromy[yy, span(g)].astype(F32)

        outrows[span(g)] = adapt[span(g)].astype(BF16)

        @pl.loop(0, GB)
        def _(i):
            other = g * GB + i

            @pl.when(other != c)
            def _():
                ret_copy(other, c).start()

    ret[c] = outrows[c]

    @pl.loop(1, C)
    def _(i):
        b = lax.rem(c - i + C, C)
        grad_copy(b, b).wait_recv()

    grads = gin[...].reshape(R, feat)
    rank_b[f] = dot(adu[...], grads, NT).astype(BF16)

    @pl.loop(1, F)
    def _(j):
        rank_copy(rank_b, bS, bR, lax.rem(f + j, F), f).start()

    @pl.loop(1, F)
    def _(j):
        other = lax.rem(f - j + F, F)
        rank_copy(rank_b, bS, bR, other, other).wait_recv()

    back = rank_b[0].astype(F32)
    for g in range(1, F):
        back = back + rank_b[g].astype(F32)
    back = (ADAPTER_SCALE * back).astype(BF16)
    lg_v[...] = dot(back, activated, NN)
    rg_v[...] = ADAPTER_SCALE * dot(low, grads, NN)

    @pl.loop(1, C)
    def _(i):
        other = lax.rem(c + i, C)
        tok_copy(other, c).wait_send()
        grad_copy(other, c).wait_send()

    @pl.loop(0, C)
    def _(b):
        @pl.loop(1, NY)
        def _(j):
            y_copy(b, lax.rem(y + j, NY), y).wait_send()

        @pl.loop(0, NY)
        def _(yy):
            k_copy(yy, b, q).wait_send()

    @pl.loop(1, F)
    def _(j):
        other = lax.rem(f + j, F)
        rank_copy(rank_b, bS, bR, other, f).wait_send()
        rank_copy(rank_l, lS, lR, other, f).wait_send()

    @pl.loop(0, NG)
    def _(g):
        @pl.loop(0, NY)
        def _(yy):
            pair_copy(yy, g, 1 - q).wait_send()

        @pl.loop(1, NY)
        def _(j):
            sum_copy(lax.rem(y + j, NY), g, y).wait_send()

    @pl.loop(1, C)
    def _(i):
        b = lax.rem(c - i + C, C)
        ret_copy(b, b).wait_recv()

    @pl.loop(1, C)
    def _(i):
        other = lax.rem(c + i, C)
        ret_copy(other, c).wait_send()


def combine_kernel(ret, wd, lg, rg, out_h, lg_h, rg_h, out, sems):
    C, _, feat = ret.shape
    left = pltpu.make_async_copy(lg, lg_h, sems.at[0])
    right = pltpu.make_async_copy(rg, rg_h, sems.at[1])
    left.start()
    right.start()
    weight = wd[...]
    high = weight.astype(BF16)
    rest = (weight - high.astype(F32)).astype(BF16)
    rows = ret[...].reshape(C * CAP, feat)
    out[...] = (dot(rows, high, TN) + dot(rows, rest, TN)).astype(BF16)
    result = pltpu.make_async_copy(out, out_h, sems.at[2])
    result.start()
    left.wait()
    right.wait()
    result.wait()


def on_device(
    tokens,
    cotangent,
    expert_indices,
    routing_weights,
    gate_up_weight_blocks,
    gate_up_block_scales,
    down_weight_blocks,
    down_block_scales,
    adapter_down_matrix,
    adapter_up_matrix,
):
    C = lax.axis_size("ctx")
    F = lax.axis_size("exp")
    NY = F // 2
    T, feat = tokens.shape
    top = expert_indices.shape[1]
    _, H, width = down_weight_blocks.shape
    rank = adapter_up_matrix.shape[1]
    R = C * CAP
    NB = width // BLOCK
    hpad = -(-H // 128) * 128
    wide = min(-(-(2 * feat + 127) // 128) * 128, width)
    bpad = -(-NB // 128) * 128
    NG = 4 if C % 4 == 0 else 1
    dma = pltpu.SemaphoreType.DMA
    scratch = [
        pltpu.VMEM((feat, T), BF16),
        pltpu.VMEM((feat, T), BF16),
        pltpu.VMEM((top, T), jnp.int32),
        pltpu.VMEM((top, T), F32),
        pltpu.VMEM((3, H, width), BF16),
        pltpu.VMEM((NB, 2, H), F32),
        pltpu.VMEM((NB, 1, H), F32),
        pltpu.VMEM((rank, H), BF16),
        pltpu.VMEM((rank, feat), BF16),
        pltpu.VMEM((bpad, hpad), F32),
        pltpu.VMEM((3, H, bpad), BF16),
        pltpu.VMEM((bpad, width), BF16),
        pltpu.VMEM((C, CAP, feat), BF16),
        pltpu.VMEM((C, CAP, feat), BF16),
        pltpu.VMEM((F, C, CAP, feat), BF16),
        pltpu.VMEM((C, CAP, feat), BF16),
        pltpu.VMEM((NY, R, wide), BF16),
        pltpu.VMEM((2, R, H), F32),
        pltpu.VMEM((R, wide), F32),
        pltpu.VMEM((F, C, CAP, feat), BF16),
        pltpu.VMEM((NY, C, CAP, feat), BF16),
        pltpu.VMEM((NY, C, CAP, feat), BF16),
        pltpu.VMEM((NY, C, CAP, feat), BF16),
        pltpu.VMEM((F, rank, R), BF16),
        pltpu.VMEM((F, rank, R), BF16),
        pltpu.VMEM((C, CAP, feat), BF16),
        pltpu.VMEM((C, CAP, feat), F32),
        dma((11,)),
        dma((C,)), dma((C,)), dma((C,)), dma((C,)), dma((C,)), dma((C,)),
        dma((NY, C)), dma((NY, C)), dma((NY, C)), dma((NY, C)),
        dma((F,)), dma((F,)), dma((F,)), dma((F,)),
        dma((NY, NG)), dma((NY, NG)), dma((NY, NG)), dma((NY, NG)),
    ]
    in_hbm = pl.BlockSpec(memory_space=pltpu.HBM)
    in_vmem = pl.BlockSpec(memory_space=pltpu.VMEM)
    mid = pl.pallas_call(
        functools.partial(block_kernel, C, F),
        out_shape=(
            jax.ShapeDtypeStruct((C, CAP, feat), BF16),
            jax.ShapeDtypeStruct((R, T), F32),
            jax.ShapeDtypeStruct((rank, H), F32),
            jax.ShapeDtypeStruct((rank, feat), F32),
        ),
        in_specs=[in_hbm] * 10,
        out_specs=(in_vmem,) * 4,
        scratch_shapes=scratch,
        compiler_params=pltpu.CompilerParams(
            collective_id=0, has_side_effects=True, vmem_limit_bytes=52 * 2**20
        ),
    )(
        *(
            pltpu.with_memory_space_constraint(x, pltpu.HBM)
            for x in (
                tokens.T,
                cotangent.T,
                expert_indices.T,
                routing_weights.T,
                gate_up_weight_blocks[0],
                jnp.transpose(gate_up_block_scales[0], (2, 0, 1)),
                down_weight_blocks[0],
                jnp.transpose(down_block_scales, (2, 0, 1)),
                adapter_down_matrix[0].T,
                adapter_up_matrix[0],
            )
        )
    )
    out_t, left_t, right = pl.pallas_call(
        combine_kernel,
        out_shape=(
            jax.ShapeDtypeStruct((feat, T), BF16),
            jax.ShapeDtypeStruct((rank, H), F32),
            jax.ShapeDtypeStruct((rank, feat), F32),
        ),
        in_specs=[in_vmem] * 4,
        out_specs=(in_hbm,) * 3,
        scratch_shapes=[pltpu.VMEM((feat, T), BF16), dma((3,))],
        compiler_params=pltpu.CompilerParams(vmem_limit_bytes=16 * 2**20),
    )(*mid)
    return out_t.T, left_t.T[None], right[None]


def solution(mesh):
    placed = (
        P("ctx", "exp"),
        P("ctx", "exp"),
        P("ctx", None),
        P("ctx", None),
        P("ctx", None, "exp", None),
        P("ctx", None, "exp", None),
        P("ctx", "exp", None),
        P("ctx", "exp", None),
        P("ctx", "exp", None),
        P("ctx", None, "exp"),
    )
    return jax.shard_map(
        on_device,
        mesh=mesh,
        in_specs=placed,
        out_specs=(P("ctx", "exp"), P("ctx", "exp", None), P("ctx", None, "exp")),
        check_vma=False,
    )
```

```python
import functools

import jax
import jax.numpy as jnp
from jax import lax
from jax.experimental import pallas as pl
from jax.experimental.pallas import tpu as pltpu
from jax.sharding import PartitionSpec as P

CAP = 16
BLOCK = 32
ADAPTER_SCALE = 0.5
GLU_ALPHA = 1.702
CLAMP_LIMIT = 7.0

F32 = jnp.float32
BF16 = jnp.bfloat16
NN = (((1,), (0,)), ((), ()))
NT = (((1,), (1,)), ((), ()))
TN = (((0,), (0,)), ((), ()))


def dot(a, b, dims):
    return lax.dot_general(a, b, dims, preferred_element_type=F32)


def unit_rows(hidden):
    for rows in (144, 128, 80, 48, 16):
        if hidden % rows == 0:
            return rows
    return hidden


def block_kernel(
    C, F,
    tok_h, cot_h, idx_h, rw_h, gu_h, gus_h, dn_h, dns_h, adl_h, adu_h,
    ret, wd, lg_v, rg_v,
    tok, cot, idx, rw, raw, gus, dns, adl, adu,
    spad, ssc, expand, rows, grows, xin, gin, xh, acc, turn,
    base, part, pair, tosend, fromy, rank_b, rank_l, outrows, adapt,
    load, tS, tR, gS, gR, rS, rR, yS, yR, kS, kR, bS, bR, lS, lR, pS, pR, qS, qR,
):
    NY = F // 2
    H, width = raw.shape[1], raw.shape[2]
    feat = tok.shape[0]
    T = tok.shape[1]
    R = C * CAP
    NB = width // BLOCK
    c = lax.axis_index("ctx")
    f = lax.axis_index("exp")
    y = f // 2
    q = f % 2
    mate = f + 1 - 2 * q

    def at_ctx(other):
        return dict(device_id=(other, f), device_id_type=pl.DeviceIdType.MESH)

    def at_exp(other):
        return dict(device_id=(c, other), device_id_type=pl.DeviceIdType.MESH)

    def paired(me, i, n):
        if n & (n - 1):
            return lax.rem(me + i, n)
        other, bit = 0, 1
        while bit < n:
            other = other + lax.rem(me // bit + i // bit, 2) * bit
            bit *= 2
        return other

    def from_pair(me, i, n):
        if n & (n - 1):
            return lax.rem(me - i + n, n)
        return paired(me, i, n)

    barrier = pltpu.get_barrier_semaphore()

    @pl.loop(1, C)
    def _(i):
        pl.semaphore_signal(barrier, inc=1, **at_ctx(lax.rem(c + i, C)))

    @pl.loop(1, F)
    def _(i):
        pl.semaphore_signal(barrier, inc=1, **at_exp(lax.rem(f + i, F)))

    loads = [
        pltpu.make_async_copy(idx_h, idx, load.at[0]),
        pltpu.make_async_copy(tok_h, tok, load.at[1]),
        pltpu.make_async_copy(rw_h, rw, load.at[2]),
        pltpu.make_async_copy(cot_h, cot, load.at[3]),
        pltpu.make_async_copy(gus_h, gus, load.at[4]),
        pltpu.make_async_copy(dns_h, dns, load.at[5]),
        pltpu.make_async_copy(gu_h.at[0], raw.at[0], load.at[6]),
        pltpu.make_async_copy(gu_h.at[1], raw.at[1], load.at[7]),
        pltpu.make_async_copy(dn_h, raw.at[2], load.at[8]),
        pltpu.make_async_copy(adl_h, adl, load.at[9]),
        pltpu.make_async_copy(adu_h, adu, load.at[10]),
    ]
    for copy in loads:
        copy.start()

    expand[...] = (
        lax.shift_right_logical(lax.broadcasted_iota(jnp.int32, expand.shape, 1), 5)
        == lax.broadcasted_iota(jnp.int32, expand.shape, 0)
    ).astype(F32).astype(BF16)
    spad[...] = jnp.zeros_like(spad)
    xh[...] = jnp.zeros_like(xh)

    loads[0].wait()
    slot = lax.broadcasted_iota(jnp.int32, (R, T), 0)
    expert = lax.shift_right_logical(slot, 4)
    number = lax.bitwise_and(slot, 15).astype(F32)
    named = idx[0:1, :] == expert
    for k in range(1, idx.shape[0]):
        named = jnp.logical_or(named, idx[k:k + 1, :] == expert)
    earlier = (
        lax.broadcasted_iota(jnp.int32, (T, T), 0) < lax.broadcasted_iota(jnp.int32, (T, T), 1)
    ).astype(F32).astype(BF16)
    position = dot(named.astype(F32).astype(BF16), earlier, NN)
    hit = jnp.logical_and(named, position == number)
    pick = hit.astype(F32).astype(BF16)
    loads[1].wait()
    rows[...] = dot(pick, tok[...], NT).astype(BF16).reshape(C, CAP, feat)

    pl.semaphore_wait(barrier, C - 1 + F - 1)

    def send_rows(src, dst, ss, rs, other, **where):
        return pltpu.make_async_remote_copy(
            src_ref=src, dst_ref=dst, send_sem=ss, recv_sem=rs, **where
        )

    def tok_copy(other, came):
        return send_rows(rows.at[other], xin.at[f, came], tS.at[other], tR.at[came], other, **at_ctx(other))

    def grad_copy(other, came):
        return send_rows(grows.at[other], gin.at[came], gS.at[other], gR.at[came], other, **at_ctx(other))

    def ret_copy(other, came):
        return send_rows(outrows.at[other], ret.at[came], rS.at[other], rR.at[came], other, **at_ctx(other))

    def y_copy(b, yy, came):
        return send_rows(
            xin.at[2 * came + q, b], xin.at[2 * came + q, b], yS.at[yy, b], yR.at[came, b], 0,
            **at_exp(2 * yy + q),
        )

    def k_copy(yy, b, core):
        return send_rows(
            xin.at[2 * yy + core, b], xin.at[2 * yy + core, b], kS.at[yy, b], kR.at[yy, b], 0,
            **at_exp(mate),
        )

    @pl.loop(1, C)
    def _(i):
        tok_copy(paired(c, C - i, C), c).start()

    xin[f, c] = rows[c]

    def forward(i):
        b = from_pair(c, i, C)

        if not isinstance(i, int):
            tok_copy(b, b).wait_recv()

        @pl.loop(1, NY)
        def _(j):
            y_copy(b, lax.rem(y + j, NY), y).start()

        k_copy(y, b, q).start()
    forward(0)

    loads[4].wait()
    loads[5].wait()
    for m in range(3):
        if m < 2:
            spad[0:NB, 0:H] = gus[:, m, :]
        else:
            spad[0:NB, 0:H] = dns[:, 0, :]
        ssc[m] = jnp.transpose(spad[...]).astype(BF16)[0:H]
    unit = unit_rows(H)
    per = H // unit
    lanes = 256

    def dequant(u):
        m = u // per
        at = pl.ds(pl.multiple_of(lax.rem(u, per) * unit, unit), unit) if per > 1 else slice(None)
        scale = ssc[m, at, :]
        for lo in range(0, width, lanes):
            hi = min(lo + lanes, width)
            spread = dot(scale, expand[:, lo:hi], NN).astype(BF16)
            raw[m, at, lo:hi] = raw[m, at, lo:hi] * spread

    def y_forward(i):
        yy = lax.rem(y - 1 - i // C + NY, NY)
        b = from_pair(c, lax.rem(i, C), C)
        y_copy(b, y, yy).wait_recv()
        k_copy(yy, b, q).start()

    units = 3 * per
    events = NY * C

    def rank_copy(buf, ss, rs, other, came):
        return send_rows(buf.at[came], buf.at[came], ss.at[other], rs.at[came], other, **at_exp(other))

    def weights_step(s):
        for m in range(3):
            @pl.when(s == m * per)
            def _():
                loads[6 + m].wait()

        @pl.when(s < units)
        def _():
            dequant(s)

    @pl.loop(0, C)
    def _(s):
        weights_step(s)

        @pl.when(s > 0)
        def _():
            forward(s)

    loads[2].wait()
    weight = jnp.zeros((R, T), F32)
    for k in range(idx.shape[0]):
        weight = weight + jnp.where(idx[k:k + 1, :] == expert, rw[k:k + 1, :], 0.0)
    weight = jnp.where(hit, weight, 0.0)
    wd[...] = weight.astype(BF16)
    loads[3].wait()
    picked = dot(pick, cot[...], NT) * jnp.sum(weight, axis=1, keepdims=True)
    grows[...] = picked.astype(BF16).reshape(C, CAP, feat)

    @pl.loop(1, C)
    def _(i):
        grad_copy(paired(c, C - i, C), c).start()

    gin[c] = grows[c]

    @pl.loop(C, max(events, units))
    def _(s):
        weights_step(s)

        @pl.when(s < events)
        def _():
            y_forward(s - C)

    def window(yy):
        lo = 2 * feat * yy // 128 * 128
        return lo, min(width, -(-2 * feat * (yy + 1) // 128) * 128)

    def arrived(yy):
        @pl.loop(0, C)
        def _(b):
            k_copy(yy, b, 1 - q).wait_recv()

    def project(yy):
        lo, hi = window(yy)
        at = 2 * feat * yy - lo
        for core in range(2):
            xh[yy, :, at:at + feat] = xin[2 * yy + core].reshape(R, feat)
            at += feat
        x = xh[yy, :, 0:hi - lo]
        return dot(raw[0, :, lo:hi], x, NT), dot(raw[1, :, lo:hi], x, NT)

    arrived(y)
    for yy in range(NY):
        @pl.when(y == yy)
        def _():
            gate_part, up_part = project(yy)
            acc[0] = gate_part
            acc[1] = up_part

    for yy in range(NY):
        @pl.when(y != yy)
        def _():
            arrived(yy)
            gate_part, up_part = project(yy)
            acc[0] += gate_part
            acc[1] += up_part

    gate = jnp.minimum(acc[0], CLAMP_LIMIT)
    up = jnp.clip(acc[1], -CLAMP_LIMIT, CLAMP_LIMIT)
    turn[0:H] = (up + 1.0) * gate / (1.0 + jnp.exp(-GLU_ALPHA * gate))
    activated = jnp.transpose(turn[...])[:, 0:H].astype(BF16)

    def columns(g):
        lo = feat * g // 128 * 128
        hi = min(width, -(-feat * (g + 1) // 128) * 128)
        at = feat * g - lo
        base[:, 0:hi - lo] = dot(activated, raw[2, :, lo:hi], NN)
        part[g] = base[:, at:at + feat].astype(BF16).reshape(C, CAP, feat)

    NG = 4 if C % 4 == 0 else 1
    GB = C // NG
    mine = c // GB

    def span(g):
        return pl.ds(g * GB, GB)

    def pair_copy(yy, g, core):
        return send_rows(
            part.at[2 * yy + core, span(g)], pair.at[yy, span(g)], pS.at[yy, g], pR.at[yy, g], 0,
            **at_exp(mate),
        )

    def sum_copy(yy, g, came):
        return send_rows(
            tosend.at[yy, span(g)], fromy.at[came, span(g)], qS.at[yy, g], qR.at[came, g], 0,
            **at_exp(2 * yy + q),
        )

    def to_mate(yy):
        @pl.loop(1, NG + 1)
        def _(n):
            pair_copy(yy, paired(mine, NG - n, NG), 1 - q).start()

    for g in range(F):
        @pl.when(jnp.logical_and(y != g // 2, q != g % 2))
        def _():
            columns(g)
            to_mate(g // 2)

    for g in range(F):
        @pl.when(jnp.logical_and(y != g // 2, q == g % 2))
        def _():
            columns(g)

    @pl.loop(1, NG + 1)
    def _(n):
        g = paired(mine, NG - n, NG)

        @pl.loop(1, NY)
        def _(j):
            yy = lax.rem(y + j, NY)
            pair_copy(yy, g, q).wait_recv()
            tosend[yy, span(g)] = (
                part[2 * yy + q, span(g)].astype(F32) + pair[yy, span(g)].astype(F32)
            ).astype(BF16)
            sum_copy(yy, g, y).start()

    for g in range(F):
        @pl.when(mate == g)
        def _():
            columns(g)
            to_mate(g // 2)

    for g in range(F):
        @pl.when(f == g)
        def _():
            columns(g)

    loads[9].wait()
    loads[10].wait()
    rank_l[f] = dot(adl[...], turn[0:H].astype(BF16), NN).astype(BF16)

    @pl.loop(1, F)
    def _(j):
        rank_copy(rank_l, lS, lR, lax.rem(f + j, F), f).start()

    @pl.loop(1, F)
    def _(j):
        other = lax.rem(f - j + F, F)
        rank_copy(rank_l, lS, lR, other, other).wait_recv()

    low = rank_l[0].astype(F32)
    for g in range(1, F):
        low = low + rank_l[g].astype(F32)
    low = low.astype(BF16)
    adapt[...] = (ADAPTER_SCALE * dot(low, adu[...], TN)).reshape(C, CAP, feat)

    @pl.loop(1, NG + 1)
    def _(n):
        g = paired(mine, NG - n, NG)
        pair_copy(y, g, q).wait_recv()
        adapt[span(g)] += part[f, span(g)].astype(F32) + pair[y, span(g)].astype(F32)

        @pl.loop(1, NY)
        def _(j):
            yy = lax.rem(y - j + NY, NY)
            sum_copy(y, g, yy).wait_recv()
            adapt[span(g)] += fromy[yy, span(g)].astype(F32)

        outrows[span(g)] = adapt[span(g)].astype(BF16)

        @pl.loop(0, GB)
        def _(i):
            other = g * GB + i

            @pl.when(other != c)
            def _():
                ret_copy(other, c).start()

    ret[c] = outrows[c]

    @pl.loop(1, C)
    def _(i):
        b = lax.rem(c - i + C, C)
        grad_copy(b, b).wait_recv()

    grads = gin[...].reshape(R, feat)
    rank_b[f] = dot(adu[...], grads, NT).astype(BF16)

    @pl.loop(1, F)
    def _(j):
        rank_copy(rank_b, bS, bR, lax.rem(f + j, F), f).start()

    @pl.loop(1, F)
    def _(j):
        other = lax.rem(f - j + F, F)
        rank_copy(rank_b, bS, bR, other, other).wait_recv()

    back = rank_b[0].astype(F32)
    for g in range(1, F):
        back = back + rank_b[g].astype(F32)
    back = (ADAPTER_SCALE * back).astype(BF16)
    lg_v[...] = dot(back, activated, NN)
    rg_v[...] = ADAPTER_SCALE * dot(low, grads, NN)

    @pl.loop(1, C)
    def _(i):
        other = lax.rem(c + i, C)
        tok_copy(other, c).wait_send()
        grad_copy(other, c).wait_send()

    @pl.loop(0, C)
    def _(b):
        @pl.loop(1, NY)
        def _(j):
            y_copy(b, lax.rem(y + j, NY), y).wait_send()

        @pl.loop(0, NY)
        def _(yy):
            k_copy(yy, b, q).wait_send()

    @pl.loop(1, F)
    def _(j):
        other = lax.rem(f + j, F)
        rank_copy(rank_b, bS, bR, other, f).wait_send()
        rank_copy(rank_l, lS, lR, other, f).wait_send()

    @pl.loop(0, NG)
    def _(g):
        @pl.loop(0, NY)
        def _(yy):
            pair_copy(yy, g, 1 - q).wait_send()

        @pl.loop(1, NY)
        def _(j):
            sum_copy(lax.rem(y + j, NY), g, y).wait_send()

    @pl.loop(1, C)
    def _(i):
        b = lax.rem(c - i + C, C)
        ret_copy(b, b).wait_recv()

    @pl.loop(1, C)
    def _(i):
        other = lax.rem(c + i, C)
        ret_copy(other, c).wait_send()


def combine_kernel(ret, wd, lg, rg, out_h, lg_h, rg_h, out, sems):
    C, _, feat = ret.shape
    left = pltpu.make_async_copy(lg, lg_h, sems.at[0])
    right = pltpu.make_async_copy(rg, rg_h, sems.at[1])
    left.start()
    right.start()
    rows = ret[...].reshape(C * CAP, feat)
    out[...] = dot(rows, wd[...], TN).astype(BF16)
    result = pltpu.make_async_copy(out, out_h, sems.at[2])
    result.start()
    left.wait()
    right.wait()
    result.wait()


def on_device(
    tokens,
    cotangent,
    expert_indices,
    routing_weights,
    gate_up_weight_blocks,
    gate_up_block_scales,
    down_weight_blocks,
    down_block_scales,
    adapter_down_matrix,
    adapter_up_matrix,
):
    C = lax.axis_size("ctx")
    F = lax.axis_size("exp")
    NY = F // 2
    T, feat = tokens.shape
    top = expert_indices.shape[1]
    _, H, width = down_weight_blocks.shape
    rank = adapter_up_matrix.shape[1]
    R = C * CAP
    NB = width // BLOCK
    hpad = -(-H // 128) * 128
    wide = min(-(-(2 * feat + 127) // 128) * 128, width)
    bpad = -(-NB // 128) * 128
    NG = 4 if C % 4 == 0 else 1
    dma = pltpu.SemaphoreType.DMA
    scratch = [
        pltpu.VMEM((feat, T), BF16),
        pltpu.VMEM((feat, T), BF16),
        pltpu.VMEM((top, T), jnp.int32),
        pltpu.VMEM((top, T), F32),
        pltpu.VMEM((3, H, width), BF16),
        pltpu.VMEM((NB, 2, H), F32),
        pltpu.VMEM((NB, 1, H), F32),
        pltpu.VMEM((rank, H), BF16),
        pltpu.VMEM((rank, feat), BF16),
        pltpu.VMEM((bpad, hpad), F32),
        pltpu.VMEM((3, H, bpad), BF16),
        pltpu.VMEM((bpad, width), BF16),
        pltpu.VMEM((C, CAP, feat), BF16),
        pltpu.VMEM((C, CAP, feat), BF16),
        pltpu.VMEM((F, C, CAP, feat), BF16),
        pltpu.VMEM((C, CAP, feat), BF16),
        pltpu.VMEM((NY, R, wide), BF16),
        pltpu.VMEM((2, H, R), F32),
        pltpu.VMEM((hpad, R), F32),
        pltpu.VMEM((R, wide), F32),
        pltpu.VMEM((F, C, CAP, feat), BF16),
        pltpu.VMEM((NY, C, CAP, feat), BF16),
        pltpu.VMEM((NY, C, CAP, feat), BF16),
        pltpu.VMEM((NY, C, CAP, feat), BF16),
        pltpu.VMEM((F, rank, R), BF16),
        pltpu.VMEM((F, rank, R), BF16),
        pltpu.VMEM((C, CAP, feat), BF16),
        pltpu.VMEM((C, CAP, feat), F32),
        dma((11,)),
        dma((C,)), dma((C,)), dma((C,)), dma((C,)), dma((C,)), dma((C,)),
        dma((NY, C)), dma((NY, C)), dma((NY, C)), dma((NY, C)),
        dma((F,)), dma((F,)), dma((F,)), dma((F,)),
        dma((NY, NG)), dma((NY, NG)), dma((NY, NG)), dma((NY, NG)),
    ]
    in_hbm = pl.BlockSpec(memory_space=pltpu.HBM)
    in_vmem = pl.BlockSpec(memory_space=pltpu.VMEM)
    mid = pl.pallas_call(
        functools.partial(block_kernel, C, F),
        out_shape=(
            jax.ShapeDtypeStruct((C, CAP, feat), BF16),
            jax.ShapeDtypeStruct((R, T), BF16),
            jax.ShapeDtypeStruct((rank, H), F32),
            jax.ShapeDtypeStruct((rank, feat), F32),
        ),
        in_specs=[in_hbm] * 10,
        out_specs=(in_vmem,) * 4,
        scratch_shapes=scratch,
        compiler_params=pltpu.CompilerParams(
            collective_id=0, has_side_effects=True, vmem_limit_bytes=52 * 2**20
        ),
    )(
        *(
            pltpu.with_memory_space_constraint(x, pltpu.HBM)
            for x in (
                tokens.T,
                cotangent.T,
                expert_indices.T,
                routing_weights.T,
                gate_up_weight_blocks[0],
                jnp.transpose(gate_up_block_scales[0], (2, 0, 1)),
                down_weight_blocks[0],
                jnp.transpose(down_block_scales, (2, 0, 1)),
                adapter_down_matrix[0].T,
                adapter_up_matrix[0],
            )
        )
    )
    out_t, left_t, right = pl.pallas_call(
        combine_kernel,
        out_shape=(
            jax.ShapeDtypeStruct((feat, T), BF16),
            jax.ShapeDtypeStruct((rank, H), F32),
            jax.ShapeDtypeStruct((rank, feat), F32),
        ),
        in_specs=[in_vmem] * 4,
        out_specs=(in_hbm,) * 3,
        scratch_shapes=[pltpu.VMEM((feat, T), BF16), dma((3,))],
        compiler_params=pltpu.CompilerParams(vmem_limit_bytes=16 * 2**20),
    )(*mid)
    return out_t.T, left_t.T[None], right[None]


def solution(mesh):
    placed = (
        P("ctx", "exp"),
        P("ctx", "exp"),
        P("ctx", None),
        P("ctx", None),
        P("ctx", None, "exp", None),
        P("ctx", None, "exp", None),
        P("ctx", "exp", None),
        P("ctx", "exp", None),
        P("ctx", "exp", None),
        P("ctx", None, "exp"),
    )
    return jax.shard_map(
        on_device,
        mesh=mesh,
        in_specs=placed,
        out_specs=(P("ctx", "exp"), P("ctx", "exp", None), P("ctx", None, "exp")),
        check_vma=False,
    )
```

```python
import functools

import jax
import jax.numpy as jnp
from jax import lax
from jax.experimental import pallas as pl
from jax.experimental.pallas import tpu as pltpu
from jax.sharding import PartitionSpec as P

CAP = 16
BLOCK = 32
ADAPTER_SCALE = 0.5
GLU_ALPHA = 1.702
CLAMP_LIMIT = 7.0

F32 = jnp.float32
BF16 = jnp.bfloat16
NN = (((1,), (0,)), ((), ()))
NT = (((1,), (1,)), ((), ()))
TN = (((0,), (0,)), ((), ()))


def dot(a, b, dims):
    return lax.dot_general(a, b, dims, preferred_element_type=F32)


def unit_rows(hidden):
    for rows in (144, 128, 80, 48, 16):
        if hidden % rows == 0:
            return rows
    return hidden


def block_kernel(
    C, F,
    tok_h, cot_h, idx_h, rw_h, gu_h, gus_h, dn_h, dns_h, adl_h, adu_h,
    ret, wd, lg_v, rg_v,
    tok, cot, idx, rw, raw, gus, dns, adl, adu,
    spad, ssc, expand, rows, grows, xin, gin, xh, act, turn,
    base, part, pair, tosend, fromy, rank_b, rank_l, outrows, adapt,
    load, tS, tR, gS, gR, rS, rR, yS, yR, kS, kR, bS, bR, lS, lR, pS, pR, qS, qR,
):
    NY = F // 2
    H, width = raw.shape[1], raw.shape[2]
    feat = tok.shape[0]
    T = tok.shape[1]
    R = C * CAP
    NB = width // BLOCK
    c = lax.axis_index("ctx")
    f = lax.axis_index("exp")
    y = f // 2
    q = f % 2
    mate = f + 1 - 2 * q

    def at_ctx(other):
        return dict(device_id=(other, f), device_id_type=pl.DeviceIdType.MESH)

    def at_exp(other):
        return dict(device_id=(c, other), device_id_type=pl.DeviceIdType.MESH)

    def paired(me, i, n):
        if n & (n - 1):
            return lax.rem(me + i, n)
        other, bit = 0, 1
        while bit < n:
            other = other + lax.rem(me // bit + i // bit, 2) * bit
            bit *= 2
        return other

    def from_pair(me, i, n):
        if n & (n - 1):
            return lax.rem(me - i + n, n)
        return paired(me, i, n)

    barrier = pltpu.get_barrier_semaphore()

    @pl.loop(1, C)
    def _(i):
        pl.semaphore_signal(barrier, inc=1, **at_ctx(lax.rem(c + i, C)))

    @pl.loop(1, F)
    def _(i):
        pl.semaphore_signal(barrier, inc=1, **at_exp(lax.rem(f + i, F)))

    loads = [
        pltpu.make_async_copy(idx_h, idx, load.at[0]),
        pltpu.make_async_copy(tok_h, tok, load.at[1]),
        pltpu.make_async_copy(rw_h, rw, load.at[2]),
        pltpu.make_async_copy(cot_h, cot, load.at[3]),
        pltpu.make_async_copy(gus_h, gus, load.at[4]),
        pltpu.make_async_copy(dns_h, dns, load.at[5]),
        pltpu.make_async_copy(gu_h.at[0], raw.at[0], load.at[6]),
        pltpu.make_async_copy(gu_h.at[1], raw.at[1], load.at[7]),
        pltpu.make_async_copy(dn_h, raw.at[2], load.at[8]),
        pltpu.make_async_copy(adl_h, adl, load.at[9]),
        pltpu.make_async_copy(adu_h, adu, load.at[10]),
    ]
    for copy in loads:
        copy.start()

    expand[...] = (
        lax.shift_right_logical(lax.broadcasted_iota(jnp.int32, expand.shape, 1), 5)
        == lax.broadcasted_iota(jnp.int32, expand.shape, 0)
    ).astype(F32).astype(BF16)
    spad[...] = jnp.zeros_like(spad)

    loads[0].wait()
    slot = lax.broadcasted_iota(jnp.int32, (R, T), 0)
    expert = lax.shift_right_logical(slot, 4)
    number = lax.bitwise_and(slot, 15).astype(F32)
    named = idx[0:1, :] == expert
    for k in range(1, idx.shape[0]):
        named = jnp.logical_or(named, idx[k:k + 1, :] == expert)
    earlier = (
        lax.broadcasted_iota(jnp.int32, (T, T), 0) < lax.broadcasted_iota(jnp.int32, (T, T), 1)
    ).astype(F32).astype(BF16)
    position = dot(named.astype(F32).astype(BF16), earlier, NN)
    hit = jnp.logical_and(named, position == number)
    pick = hit.astype(F32).astype(BF16)
    loads[1].wait()
    rows[...] = dot(pick, tok[...], NT).astype(BF16).reshape(C, CAP, feat)

    pl.semaphore_wait(barrier, C - 1 + F - 1)

    def send_rows(src, dst, ss, rs, other, **where):
        return pltpu.make_async_remote_copy(
            src_ref=src, dst_ref=dst, send_sem=ss, recv_sem=rs, **where
        )

    def tok_copy(other, came):
        return send_rows(rows.at[other], xin.at[f, came], tS.at[other], tR.at[came], other, **at_ctx(other))

    def grad_copy(other, came):
        return send_rows(grows.at[other], gin.at[came], gS.at[other], gR.at[came], other, **at_ctx(other))

    def ret_copy(other, came):
        return send_rows(outrows.at[other], ret.at[came], rS.at[other], rR.at[came], other, **at_ctx(other))

    def y_copy(b, yy, came):
        return send_rows(
            xin.at[2 * came + q, b], xin.at[2 * came + q, b], yS.at[yy, b], yR.at[came, b], 0,
            **at_exp(2 * yy + q),
        )

    def k_copy(yy, b, core):
        return send_rows(
            xin.at[2 * yy + core, b], xin.at[2 * yy + core, b], kS.at[yy, b], kR.at[yy, b], 0,
            **at_exp(mate),
        )

    @pl.loop(1, C)
    def _(i):
        tok_copy(paired(c, C - i, C), c).start()

    xin[f, c] = rows[c]

    def forward(i):
        b = from_pair(c, i, C)

        if not isinstance(i, int):
            tok_copy(b, b).wait_recv()

        @pl.loop(1, NY)
        def _(j):
            y_copy(b, lax.rem(y + j, NY), y).start()

        k_copy(y, b, q).start()
    forward(0)

    loads[4].wait()
    loads[5].wait()
    for m in range(3):
        if m < 2:
            spad[0:NB, 0:H] = gus[:, m, :]
        else:
            spad[0:NB, 0:H] = dns[:, 0, :]
        ssc[m] = jnp.transpose(spad[...]).astype(BF16)[0:H]
    unit = unit_rows(H)
    per = H // unit
    lanes = 256

    def dequant(u):
        m = u // per
        at = pl.ds(pl.multiple_of(lax.rem(u, per) * unit, unit), unit) if per > 1 else slice(None)
        scale = ssc[m, at, :]
        for lo in range(0, width, lanes):
            hi = min(lo + lanes, width)
            spread = dot(scale, expand[:, lo:hi], NN).astype(BF16)
            raw[m, at, lo:hi] = raw[m, at, lo:hi] * spread

    def y_forward(i):
        yy = lax.rem(y - 1 - i // C + NY, NY)
        b = from_pair(c, lax.rem(i, C), C)
        y_copy(b, y, yy).wait_recv()
        k_copy(yy, b, q).start()

    units = 3 * per
    events = NY * C

    def rank_copy(buf, ss, rs, other, came):
        return send_rows(buf.at[came], buf.at[came], ss.at[other], rs.at[came], other, **at_exp(other))

    def weights_step(s):
        for m in range(3):
            @pl.when(s == m * per)
            def _():
                loads[6 + m].wait()

        @pl.when(s < units)
        def _():
            dequant(s)

    @pl.loop(0, max(events, units))
    def _(s):
        weights_step(s)

        @pl.when(jnp.logical_and(s > 0, s < C))
        def _():
            forward(s)

        @pl.when(s == C)
        def _():
            loads[2].wait()
            weight = jnp.zeros((R, T), F32)
            for k in range(idx.shape[0]):
                weight = weight + jnp.where(idx[k:k + 1, :] == expert, rw[k:k + 1, :], 0.0)
            weight = jnp.where(hit, weight, 0.0)
            wd[...] = weight.astype(BF16)
            loads[3].wait()
            picked = dot(pick, cot[...], NT) * jnp.sum(weight, axis=1, keepdims=True)
            grows[...] = picked.astype(BF16).reshape(C, CAP, feat)

            @pl.loop(1, C)
            def _(i):
                grad_copy(paired(c, C - i, C), c).start()

            gin[c] = grows[c]

        @pl.when(jnp.logical_and(s >= C, s < events))
        def _():
            y_forward(s - C)

    @pl.loop(0, NY)
    def _(yy):
        @pl.loop(0, C)
        def _(b):
            k_copy(yy, b, 1 - q).wait_recv()

    for g in range(F):
        xh[:, g * feat:(g + 1) * feat] = xin[g].reshape(R, feat)

    tall = 240 if H % 240 == 0 else H

    @pl.loop(0, H // tall)
    def _(i):
        at = pl.ds(pl.multiple_of(i * tall, tall), tall) if tall < H else slice(None)
        x = xh[...]
        gate = jnp.minimum(dot(raw[0, at, :], x, NT), CLAMP_LIMIT)
        up = jnp.clip(dot(raw[1, at, :], x, NT), -CLAMP_LIMIT, CLAMP_LIMIT)
        turn[at if tall < H else slice(0, H)] = (up + 1.0) * gate / (1.0 + jnp.exp(-GLU_ALPHA * gate))

    act[...] = jnp.transpose(turn[...])[:, 0:H].astype(BF16)
    activated = act[...]

    @pl.loop(0, width // lanes)
    def _(n):
        at = pl.ds(pl.multiple_of(n * lanes, lanes), lanes)
        base[:, at] = dot(act[...], raw[2, :, at], NN)

    if width % lanes:
        last = width // lanes * lanes
        base[:, last:width] = dot(act[...], raw[2, :, last:width], NN)
    for g in range(F):
        part[g] = base[:, g * feat:(g + 1) * feat].astype(BF16).reshape(C, CAP, feat)

    NG = 4 if C % 4 == 0 else 1
    GB = C // NG
    mine = c // GB

    def span(g):
        return pl.ds(g * GB, GB)

    def pair_copy(yy, g, core):
        return send_rows(
            part.at[2 * yy + core, span(g)], pair.at[yy, span(g)], pS.at[yy, g], pR.at[yy, g], 0,
            **at_exp(mate),
        )

    def sum_copy(yy, g, came):
        return send_rows(
            tosend.at[yy, span(g)], fromy.at[came, span(g)], qS.at[yy, g], qR.at[came, g], 0,
            **at_exp(2 * yy + q),
        )

    def to_mate(yy):
        @pl.loop(1, NG + 1)
        def _(n):
            pair_copy(yy, paired(mine, NG - n, NG), 1 - q).start()

    @pl.loop(1, NY + 1)
    def _(j):
        to_mate(lax.rem(y + j, NY))

    @pl.loop(1, NG + 1)
    def _(n):
        g = paired(mine, NG - n, NG)

        @pl.loop(1, NY)
        def _(j):
            yy = lax.rem(y + j, NY)
            pair_copy(yy, g, q).wait_recv()
            tosend[yy, span(g)] = (
                part[2 * yy + q, span(g)].astype(F32) + pair[yy, span(g)].astype(F32)
            ).astype(BF16)
            sum_copy(yy, g, y).start()

    loads[9].wait()
    loads[10].wait()
    rank_l[f] = dot(adl[...], turn[0:H].astype(BF16), NN).astype(BF16)

    @pl.loop(1, F)
    def _(j):
        rank_copy(rank_l, lS, lR, lax.rem(f + j, F), f).start()

    @pl.loop(1, F)
    def _(j):
        other = lax.rem(f - j + F, F)
        rank_copy(rank_l, lS, lR, other, other).wait_recv()

    low = rank_l[0].astype(F32)
    for g in range(1, F):
        low = low + rank_l[g].astype(F32)
    low = low.astype(BF16)
    adapt[...] = (ADAPTER_SCALE * dot(low, adu[...], TN)).reshape(C, CAP, feat)

    @pl.loop(1, NG + 1)
    def _(n):
        g = paired(mine, NG - n, NG)
        pair_copy(y, g, q).wait_recv()
        adapt[span(g)] += part[f, span(g)].astype(F32) + pair[y, span(g)].astype(F32)

        @pl.loop(1, NY)
        def _(j):
            yy = lax.rem(y - j + NY, NY)
            sum_copy(y, g, yy).wait_recv()
            adapt[span(g)] += fromy[yy, span(g)].astype(F32)

        outrows[span(g)] = adapt[span(g)].astype(BF16)

        @pl.loop(0, GB)
        def _(i):
            other = g * GB + i

            @pl.when(other != c)
            def _():
                ret_copy(other, c).start()

    ret[c] = outrows[c]

    @pl.loop(1, C)
    def _(i):
        b = lax.rem(c - i + C, C)
        grad_copy(b, b).wait_recv()

    grads = gin[...].reshape(R, feat)
    rank_b[f] = dot(adu[...], grads, NT).astype(BF16)

    @pl.loop(1, F)
    def _(j):
        rank_copy(rank_b, bS, bR, lax.rem(f + j, F), f).start()

    @pl.loop(1, F)
    def _(j):
        other = lax.rem(f - j + F, F)
        rank_copy(rank_b, bS, bR, other, other).wait_recv()

    back = rank_b[0].astype(F32)
    for g in range(1, F):
        back = back + rank_b[g].astype(F32)
    back = (ADAPTER_SCALE * back).astype(BF16)
    lg_v[...] = dot(back, activated, NN)
    rg_v[...] = ADAPTER_SCALE * dot(low, grads, NN)

    @pl.loop(1, C)
    def _(i):
        other = lax.rem(c + i, C)
        tok_copy(other, c).wait_send()
        grad_copy(other, c).wait_send()

    @pl.loop(0, C)
    def _(b):
        @pl.loop(1, NY)
        def _(j):
            y_copy(b, lax.rem(y + j, NY), y).wait_send()

        @pl.loop(0, NY)
        def _(yy):
            k_copy(yy, b, q).wait_send()

    @pl.loop(1, F)
    def _(j):
        other = lax.rem(f + j, F)
        rank_copy(rank_b, bS, bR, other, f).wait_send()
        rank_copy(rank_l, lS, lR, other, f).wait_send()

    @pl.loop(0, NG)
    def _(g):
        @pl.loop(0, NY)
        def _(yy):
            pair_copy(yy, g, 1 - q).wait_send()

        @pl.loop(1, NY)
        def _(j):
            sum_copy(lax.rem(y + j, NY), g, y).wait_send()

    @pl.loop(1, C)
    def _(i):
        b = lax.rem(c - i + C, C)
        ret_copy(b, b).wait_recv()

    @pl.loop(1, C)
    def _(i):
        other = lax.rem(c + i, C)
        ret_copy(other, c).wait_send()


def combine_kernel(ret, wd, lg, rg, out_h, lg_h, rg_h, out, sems):
    C, _, feat = ret.shape
    left = pltpu.make_async_copy(lg, lg_h, sems.at[0])
    right = pltpu.make_async_copy(rg, rg_h, sems.at[1])
    left.start()
    right.start()
    rows = ret[...].reshape(C * CAP, feat)
    out[...] = dot(rows, wd[...], TN).astype(BF16)
    result = pltpu.make_async_copy(out, out_h, sems.at[2])
    result.start()
    left.wait()
    right.wait()
    result.wait()


def on_device(
    tokens,
    cotangent,
    expert_indices,
    routing_weights,
    gate_up_weight_blocks,
    gate_up_block_scales,
    down_weight_blocks,
    down_block_scales,
    adapter_down_matrix,
    adapter_up_matrix,
):
    C = lax.axis_size("ctx")
    F = lax.axis_size("exp")
    NY = F // 2
    T, feat = tokens.shape
    top = expert_indices.shape[1]
    _, H, width = down_weight_blocks.shape
    rank = adapter_up_matrix.shape[1]
    R = C * CAP
    NB = width // BLOCK
    hpad = -(-H // 128) * 128
    bpad = -(-NB // 128) * 128
    NG = 4 if C % 4 == 0 else 1
    dma = pltpu.SemaphoreType.DMA
    scratch = [
        pltpu.VMEM((feat, T), BF16),
        pltpu.VMEM((feat, T), BF16),
        pltpu.VMEM((top, T), jnp.int32),
        pltpu.VMEM((top, T), F32),
        pltpu.VMEM((3, H, width), BF16),
        pltpu.VMEM((NB, 2, H), F32),
        pltpu.VMEM((NB, 1, H), F32),
        pltpu.VMEM((rank, H), BF16),
        pltpu.VMEM((rank, feat), BF16),
        pltpu.VMEM((bpad, hpad), F32),
        pltpu.VMEM((3, H, bpad), BF16),
        pltpu.VMEM((bpad, width), BF16),
        pltpu.VMEM((C, CAP, feat), BF16),
        pltpu.VMEM((C, CAP, feat), BF16),
        pltpu.VMEM((F, C, CAP, feat), BF16),
        pltpu.VMEM((C, CAP, feat), BF16),
        pltpu.VMEM((R, width), BF16),
        pltpu.VMEM((R, H), BF16),
        pltpu.VMEM((hpad, R), F32),
        pltpu.VMEM((R, width), F32),
        pltpu.VMEM((F, C, CAP, feat), BF16),
        pltpu.VMEM((NY, C, CAP, feat), BF16),
        pltpu.VMEM((NY, C, CAP, feat), BF16),
        pltpu.VMEM((NY, C, CAP, feat), BF16),
        pltpu.VMEM((F, rank, R), BF16),
        pltpu.VMEM((F, rank, R), BF16),
        pltpu.VMEM((C, CAP, feat), BF16),
        pltpu.VMEM((C, CAP, feat), F32),
        dma((11,)),
        dma((C,)), dma((C,)), dma((C,)), dma((C,)), dma((C,)), dma((C,)),
        dma((NY, C)), dma((NY, C)), dma((NY, C)), dma((NY, C)),
        dma((F,)), dma((F,)), dma((F,)), dma((F,)),
        dma((NY, NG)), dma((NY, NG)), dma((NY, NG)), dma((NY, NG)),
    ]
    in_hbm = pl.BlockSpec(memory_space=pltpu.HBM)
    in_vmem = pl.BlockSpec(memory_space=pltpu.VMEM)
    mid = pl.pallas_call(
        functools.partial(block_kernel, C, F),
        out_shape=(
            jax.ShapeDtypeStruct((C, CAP, feat), BF16),
            jax.ShapeDtypeStruct((R, T), BF16),
            jax.ShapeDtypeStruct((rank, H), F32),
            jax.ShapeDtypeStruct((rank, feat), F32),
        ),
        in_specs=[in_hbm] * 10,
        out_specs=(in_vmem,) * 4,
        scratch_shapes=scratch,
        compiler_params=pltpu.CompilerParams(
            collective_id=0, has_side_effects=True, vmem_limit_bytes=52 * 2**20
        ),
    )(
        *(
            pltpu.with_memory_space_constraint(x, pltpu.HBM)
            for x in (
                tokens.T,
                cotangent.T,
                expert_indices.T,
                routing_weights.T,
                gate_up_weight_blocks[0],
                jnp.transpose(gate_up_block_scales[0], (2, 0, 1)),
                down_weight_blocks[0],
                jnp.transpose(down_block_scales, (2, 0, 1)),
                adapter_down_matrix[0].T,
                adapter_up_matrix[0],
            )
        )
    )
    out_t, left_t, right = pl.pallas_call(
        combine_kernel,
        out_shape=(
            jax.ShapeDtypeStruct((feat, T), BF16),
            jax.ShapeDtypeStruct((rank, H), F32),
            jax.ShapeDtypeStruct((rank, feat), F32),
        ),
        in_specs=[in_vmem] * 4,
        out_specs=(in_hbm,) * 3,
        scratch_shapes=[pltpu.VMEM((feat, T), BF16), dma((3,))],
        compiler_params=pltpu.CompilerParams(vmem_limit_bytes=16 * 2**20),
    )(*mid)
    return out_t.T, left_t.T[None], right[None]


def solution(mesh):
    placed = (
        P("ctx", "exp"),
        P("ctx", "exp"),
        P("ctx", None),
        P("ctx", None),
        P("ctx", None, "exp", None),
        P("ctx", None, "exp", None),
        P("ctx", "exp", None),
        P("ctx", "exp", None),
        P("ctx", "exp", None),
        P("ctx", None, "exp"),
    )
    return jax.shard_map(
        on_device,
        mesh=mesh,
        in_specs=placed,
        out_specs=(P("ctx", "exp"), P("ctx", "exp", None), P("ctx", None, "exp")),
        check_vma=False,
    )
```

```python
import functools

import jax
import jax.numpy as jnp
from jax import lax
from jax.experimental import pallas as pl
from jax.experimental.pallas import tpu as pltpu
from jax.sharding import PartitionSpec as P

CAP = 16
BLOCK = 32
ADAPTER_SCALE = 0.5
GLU_ALPHA = 1.702
CLAMP_LIMIT = 7.0

F32 = jnp.float32
BF16 = jnp.bfloat16
NN = (((1,), (0,)), ((), ()))
NT = (((1,), (1,)), ((), ()))
TN = (((0,), (0,)), ((), ()))


def dot(a, b, dims):
    return lax.dot_general(a, b, dims, preferred_element_type=F32)


def unit_rows(hidden):
    for rows in (144, 128, 80, 48, 16):
        if hidden % rows == 0:
            return rows
    return hidden


def block_kernel(
    C, F,
    tok_h, cot_h, idx_h, rw_h, gu_h, gus_h, dn_h, dns_h, adl_h, adu_h,
    ret, wd, lg_v, rg_v,
    tok, cot, idx, rw, raw, gus, dns, adl, adu,
    spad, ssc, expand, rows, grows, xin, gin, xh, acc,
    base, part, pair, tosend, fromy, rank_b, rank_l, outrows, adapt,
    load, tS, tR, gS, gR, rS, rR, yS, yR, kS, kR, bS, bR, lS, lR, pS, pR, qS, qR,
):
    NY = F // 2
    H, width = raw.shape[1], raw.shape[2]
    feat = tok.shape[0]
    T = tok.shape[1]
    R = C * CAP
    NB = width // BLOCK
    c = lax.axis_index("ctx")
    f = lax.axis_index("exp")
    y = f // 2
    q = f % 2
    mate = f + 1 - 2 * q

    def at_ctx(other):
        return dict(device_id=(other, f), device_id_type=pl.DeviceIdType.MESH)

    def at_exp(other):
        return dict(device_id=(c, other), device_id_type=pl.DeviceIdType.MESH)

    def paired(me, i, n):
        if n & (n - 1):
            return lax.rem(me + i, n)
        other, bit = 0, 1
        while bit < n:
            other = other + lax.rem(me // bit + i // bit, 2) * bit
            bit *= 2
        return other

    def from_pair(me, i, n):
        if n & (n - 1):
            return lax.rem(me - i + n, n)
        return paired(me, i, n)

    barrier = pltpu.get_barrier_semaphore()

    @pl.loop(1, C)
    def _(i):
        pl.semaphore_signal(barrier, inc=1, **at_ctx(lax.rem(c + i, C)))

    @pl.loop(1, F)
    def _(i):
        pl.semaphore_signal(barrier, inc=1, **at_exp(lax.rem(f + i, F)))

    loads = [
        pltpu.make_async_copy(idx_h, idx, load.at[0]),
        pltpu.make_async_copy(tok_h, tok, load.at[1]),
        pltpu.make_async_copy(rw_h, rw, load.at[2]),
        pltpu.make_async_copy(cot_h, cot, load.at[3]),
        pltpu.make_async_copy(gus_h, gus, load.at[4]),
        pltpu.make_async_copy(dns_h, dns, load.at[5]),
        pltpu.make_async_copy(gu_h.at[0], raw.at[0], load.at[6]),
        pltpu.make_async_copy(gu_h.at[1], raw.at[1], load.at[7]),
        pltpu.make_async_copy(dn_h, raw.at[2], load.at[8]),
        pltpu.make_async_copy(adl_h, adl, load.at[9]),
        pltpu.make_async_copy(adu_h, adu, load.at[10]),
    ]
    for copy in loads:
        copy.start()

    expand[...] = (
        lax.shift_right_logical(lax.broadcasted_iota(jnp.int32, expand.shape, 1), 5)
        == lax.broadcasted_iota(jnp.int32, expand.shape, 0)
    ).astype(F32).astype(BF16)
    spad[...] = jnp.zeros_like(spad)
    xh[...] = jnp.zeros_like(xh)

    loads[0].wait()
    slot = lax.broadcasted_iota(jnp.int32, (R, T), 0)
    expert = lax.shift_right_logical(slot, 4)
    number = lax.bitwise_and(slot, 15).astype(F32)
    named = idx[0:1, :] == expert
    for k in range(1, idx.shape[0]):
        named = jnp.logical_or(named, idx[k:k + 1, :] == expert)
    earlier = (
        lax.broadcasted_iota(jnp.int32, (T, T), 0) < lax.broadcasted_iota(jnp.int32, (T, T), 1)
    ).astype(F32).astype(BF16)
    position = dot(named.astype(F32).astype(BF16), earlier, NN)
    hit = jnp.logical_and(named, position == number)
    pick = hit.astype(F32).astype(BF16)
    loads[1].wait()
    rows[...] = dot(pick, tok[...], NT).astype(BF16).reshape(C, CAP, feat)

    pl.semaphore_wait(barrier, C - 1 + F - 1)

    def send_rows(src, dst, ss, rs, other, **where):
        return pltpu.make_async_remote_copy(
            src_ref=src, dst_ref=dst, send_sem=ss, recv_sem=rs, **where
        )

    def tok_copy(other, came):
        return send_rows(rows.at[other], xin.at[f, came], tS.at[other], tR.at[came], other, **at_ctx(other))

    def grad_copy(other, came):
        return send_rows(grows.at[other], gin.at[came], gS.at[other], gR.at[came], other, **at_ctx(other))

    def ret_copy(other, came):
        return send_rows(outrows.at[other], ret.at[came], rS.at[other], rR.at[came], other, **at_ctx(other))

    def y_copy(b, yy, came):
        return send_rows(
            xin.at[2 * came + q, b], xin.at[2 * came + q, b], yS.at[yy, b], yR.at[came, b], 0,
            **at_exp(2 * yy + q),
        )

    def k_copy(yy, b, core):
        return send_rows(
            xin.at[2 * yy + core, b], xin.at[2 * yy + core, b], kS.at[yy, b], kR.at[yy, b], 0,
            **at_exp(mate),
        )

    @pl.loop(1, C)
    def _(i):
        tok_copy(paired(c, C - i, C), c).start()

    xin[f, c] = rows[c]

    def forward(i):
        b = from_pair(c, i, C)

        if not isinstance(i, int):
            tok_copy(b, b).wait_recv()

        @pl.loop(1, NY)
        def _(j):
            y_copy(b, lax.rem(y + j, NY), y).start()

        k_copy(y, b, q).start()
    forward(0)

    loads[4].wait()
    loads[5].wait()
    for m in range(3):
        if m < 2:
            spad[0:NB, 0:H] = gus[:, m, :]
        else:
            spad[0:NB, 0:H] = dns[:, 0, :]
        ssc[m] = jnp.transpose(spad[...])[0:H]
    unit = unit_rows(H)
    per = H // unit
    lanes = 256

    def dequant(u):
        m = u // per
        at = pl.ds(pl.multiple_of(lax.rem(u, per) * unit, unit), unit) if per > 1 else slice(None)
        scale = ssc[m, at, :]
        narrow = scale.astype(BF16)
        lane = lax.shift_right_logical(lax.broadcasted_iota(jnp.int32, scale.shape, 1), 5)
        for lo in range(0, width, lanes):
            hi = min(lo + lanes, width)
            if lo // lanes % 3 == 2 and hi - lo == lanes:
                for at_lane in range(lo, hi, 128):
                    here = slice(at_lane, at_lane + 128)
                    spread = jnp.take_along_axis(scale, lane + at_lane // BLOCK, axis=1).astype(BF16)
                    raw[m, at, here] = raw[m, at, here] * spread
            else:
                spread = dot(narrow, expand[:, lo:hi], NN).astype(BF16)
                raw[m, at, lo:hi] = raw[m, at, lo:hi] * spread

    def y_forward(i):
        yy = lax.rem(y - 1 - i // C + NY, NY)
        b = from_pair(c, lax.rem(i, C), C)
        y_copy(b, y, yy).wait_recv()
        k_copy(yy, b, q).start()

    units = 3 * per
    events = NY * C

    @pl.loop(0, max(events, units))
    def _(s):
        for m in range(3):
            @pl.when(s == m * per)
            def _():
                loads[6 + m].wait()

        @pl.when(s < units)
        def _():
            dequant(s)

        @pl.when(jnp.logical_and(s > 0, s < C))
        def _():
            forward(s)

        @pl.when(s == C)
        def _():
            loads[2].wait()
            weight = jnp.zeros((R, T), F32)
            for k in range(idx.shape[0]):
                weight = weight + jnp.where(idx[k:k + 1, :] == expert, rw[k:k + 1, :], 0.0)
            weight = jnp.where(hit, weight, 0.0)
            wd[...] = weight.astype(BF16)
            loads[3].wait()
            picked = dot(pick, cot[...], NT) * jnp.sum(weight, axis=1, keepdims=True)
            grows[...] = picked.astype(BF16).reshape(C, CAP, feat)

            @pl.loop(1, C)
            def _(i):
                grad_copy(paired(c, C - i, C), c).start()

            gin[c] = grows[c]

        @pl.when(jnp.logical_and(s >= C, s < events))
        def _():
            y_forward(s - C)

    def rank_copy(buf, ss, rs, other, came):
        return send_rows(buf.at[came], buf.at[came], ss.at[other], rs.at[came], other, **at_exp(other))

    def window(yy):
        lo = 2 * feat * yy // 128 * 128
        return lo, min(width, -(-2 * feat * (yy + 1) // 128) * 128)

    def arrived(yy):
        @pl.loop(0, C)
        def _(b):
            k_copy(yy, b, 1 - q).wait_recv()

    def project(yy):
        lo, hi = window(yy)
        at = 2 * feat * yy - lo
        for core in range(2):
            xh[yy, :, at:at + feat] = xin[2 * yy + core].reshape(R, feat)
            at += feat
        x = xh[yy, :, 0:hi - lo]
        return dot(x, raw[0, :, lo:hi], NT), dot(x, raw[1, :, lo:hi], NT)

    arrived(y)
    for yy in range(NY):
        @pl.when(y == yy)
        def _():
            gate_part, up_part = project(yy)
            acc[0] = gate_part
            acc[1] = up_part

    for yy in range(NY):
        @pl.when(y != yy)
        def _():
            arrived(yy)
            gate_part, up_part = project(yy)
            acc[0] += gate_part
            acc[1] += up_part

    gate = jnp.minimum(acc[0], CLAMP_LIMIT)
    up = jnp.clip(acc[1], -CLAMP_LIMIT, CLAMP_LIMIT)
    activated = ((up + 1.0) * gate / (1.0 + jnp.exp(-GLU_ALPHA * gate))).astype(BF16)

    loads[9].wait()
    loads[10].wait()
    rank_l[f] = dot(adl[...], activated, NT).astype(BF16)

    @pl.loop(1, F)
    def _(j):
        rank_copy(rank_l, lS, lR, lax.rem(f + j, F), f).start()

    def columns(yy):
        lo, hi = window(yy)
        base[:, 0:hi - lo] = dot(activated, raw[2, :, lo:hi], NN)
        at = 2 * feat * yy - lo
        for core in range(2):
            part[2 * yy + core] = base[:, at:at + feat].astype(BF16).reshape(C, CAP, feat)
            at += feat

    NG = 4 if C % 4 == 0 else 1
    GB = C // NG
    mine = c // GB

    def span(g):
        return pl.ds(g * GB, GB)

    def pair_copy(yy, g, core):
        return send_rows(
            part.at[2 * yy + core, span(g)], pair.at[yy, span(g)], pS.at[yy, g], pR.at[yy, g], 0,
            **at_exp(mate),
        )

    def sum_copy(yy, g, came):
        return send_rows(
            tosend.at[yy, span(g)], fromy.at[came, span(g)], qS.at[yy, g], qR.at[came, g], 0,
            **at_exp(2 * yy + q),
        )

    def to_mate(yy):
        @pl.loop(1, NG + 1)
        def _(n):
            pair_copy(yy, paired(mine, NG - n, NG), 1 - q).start()

    for yy in range(NY):
        @pl.when(y != yy)
        def _():
            columns(yy)
            to_mate(yy)

    @pl.loop(1, NG + 1)
    def _(n):
        g = paired(mine, NG - n, NG)

        @pl.loop(1, NY)
        def _(j):
            yy = lax.rem(y + j, NY)
            pair_copy(yy, g, q).wait_recv()
            tosend[yy, span(g)] = (
                part[2 * yy + q, span(g)].astype(F32) + pair[yy, span(g)].astype(F32)
            ).astype(BF16)
            sum_copy(yy, g, y).start()

    for yy in range(NY):
        @pl.when(y == yy)
        def _():
            columns(yy)
            to_mate(yy)

    @pl.loop(1, F)
    def _(j):
        other = lax.rem(f - j + F, F)
        rank_copy(rank_l, lS, lR, other, other).wait_recv()

    low = rank_l[0].astype(F32)
    for g in range(1, F):
        low = low + rank_l[g].astype(F32)
    low = low.astype(BF16)
    adapt[...] = (ADAPTER_SCALE * dot(low, adu[...], TN)).reshape(C, CAP, feat)

    @pl.loop(1, NG + 1)
    def _(n):
        g = paired(mine, NG - n, NG)
        pair_copy(y, g, q).wait_recv()
        adapt[span(g)] += part[f, span(g)].astype(F32) + pair[y, span(g)].astype(F32)

        @pl.loop(1, NY)
        def _(j):
            yy = lax.rem(y - j + NY, NY)
            sum_copy(y, g, yy).wait_recv()
            adapt[span(g)] += fromy[yy, span(g)].astype(F32)

        outrows[span(g)] = adapt[span(g)].astype(BF16)

        @pl.loop(0, GB)
        def _(i):
            other = g * GB + i

            @pl.when(other != c)
            def _():
                ret_copy(other, c).start()

    ret[c] = outrows[c]

    @pl.loop(1, C)
    def _(i):
        b = lax.rem(c - i + C, C)
        grad_copy(b, b).wait_recv()

    grads = gin[...].reshape(R, feat)
    rank_b[f] = dot(adu[...], grads, NT).astype(BF16)

    @pl.loop(1, F)
    def _(j):
        rank_copy(rank_b, bS, bR, lax.rem(f + j, F), f).start()

    @pl.loop(1, F)
    def _(j):
        other = lax.rem(f - j + F, F)
        rank_copy(rank_b, bS, bR, other, other).wait_recv()

    back = rank_b[0].astype(F32)
    for g in range(1, F):
        back = back + rank_b[g].astype(F32)
    back = (ADAPTER_SCALE * back).astype(BF16)
    lg_v[...] = dot(back, activated, NN)
    rg_v[...] = ADAPTER_SCALE * dot(low, grads, NN)

    @pl.loop(1, C)
    def _(i):
        other = lax.rem(c + i, C)
        tok_copy(other, c).wait_send()
        grad_copy(other, c).wait_send()

    @pl.loop(0, C)
    def _(b):
        @pl.loop(1, NY)
        def _(j):
            y_copy(b, lax.rem(y + j, NY), y).wait_send()

        @pl.loop(0, NY)
        def _(yy):
            k_copy(yy, b, q).wait_send()

    @pl.loop(1, F)
    def _(j):
        other = lax.rem(f + j, F)
        rank_copy(rank_b, bS, bR, other, f).wait_send()
        rank_copy(rank_l, lS, lR, other, f).wait_send()

    @pl.loop(0, NG)
    def _(g):
        @pl.loop(0, NY)
        def _(yy):
            pair_copy(yy, g, 1 - q).wait_send()

        @pl.loop(1, NY)
        def _(j):
            sum_copy(lax.rem(y + j, NY), g, y).wait_send()

    @pl.loop(1, C)
    def _(i):
        b = lax.rem(c - i + C, C)
        ret_copy(b, b).wait_recv()

    @pl.loop(1, C)
    def _(i):
        other = lax.rem(c + i, C)
        ret_copy(other, c).wait_send()


def combine_kernel(ret, wd, lg, rg, out_h, lg_h, rg_h, out, sems):
    C, _, feat = ret.shape
    left = pltpu.make_async_copy(lg, lg_h, sems.at[0])
    right = pltpu.make_async_copy(rg, rg_h, sems.at[1])
    left.start()
    right.start()
    rows = ret[...].reshape(C * CAP, feat)
    out[...] = dot(rows, wd[...], TN).astype(BF16)
    result = pltpu.make_async_copy(out, out_h, sems.at[2])
    result.start()
    left.wait()
    right.wait()
    result.wait()


def on_device(
    tokens,
    cotangent,
    expert_indices,
    routing_weights,
    gate_up_weight_blocks,
    gate_up_block_scales,
    down_weight_blocks,
    down_block_scales,
    adapter_down_matrix,
    adapter_up_matrix,
):
    C = lax.axis_size("ctx")
    F = lax.axis_size("exp")
    NY = F // 2
    T, feat = tokens.shape
    top = expert_indices.shape[1]
    _, H, width = down_weight_blocks.shape
    rank = adapter_up_matrix.shape[1]
    R = C * CAP
    NB = width // BLOCK
    hpad = -(-H // 128) * 128
    wide = min(-(-(2 * feat + 127) // 128) * 128, width)
    bpad = -(-NB // 128) * 128
    NG = 4 if C % 4 == 0 else 1
    dma = pltpu.SemaphoreType.DMA
    scratch = [
        pltpu.VMEM((feat, T), BF16),
        pltpu.VMEM((feat, T), BF16),
        pltpu.VMEM((top, T), jnp.int32),
        pltpu.VMEM((top, T), F32),
        pltpu.VMEM((3, H, width), BF16),
        pltpu.VMEM((NB, 2, H), F32),
        pltpu.VMEM((NB, 1, H), F32),
        pltpu.VMEM((rank, H), BF16),
        pltpu.VMEM((rank, feat), BF16),
        pltpu.VMEM((bpad, hpad), F32),
        pltpu.VMEM((3, H, bpad), F32),
        pltpu.VMEM((bpad, width), BF16),
        pltpu.VMEM((C, CAP, feat), BF16),
        pltpu.VMEM((C, CAP, feat), BF16),
        pltpu.VMEM((F, C, CAP, feat), BF16),
        pltpu.VMEM((C, CAP, feat), BF16),
        pltpu.VMEM((NY, R, wide), BF16),
        pltpu.VMEM((2, R, H), F32),
        pltpu.VMEM((R, wide), F32),
        pltpu.VMEM((F, C, CAP, feat), BF16),
        pltpu.VMEM((NY, C, CAP, feat), BF16),
        pltpu.VMEM((NY, C, CAP, feat), BF16),
        pltpu.VMEM((NY, C, CAP, feat), BF16),
        pltpu.VMEM((F, rank, R), BF16),
        pltpu.VMEM((F, rank, R), BF16),
        pltpu.VMEM((C, CAP, feat), BF16),
        pltpu.VMEM((C, CAP, feat), F32),
        dma((11,)),
        dma((C,)), dma((C,)), dma((C,)), dma((C,)), dma((C,)), dma((C,)),
        dma((NY, C)), dma((NY, C)), dma((NY, C)), dma((NY, C)),
        dma((F,)), dma((F,)), dma((F,)), dma((F,)),
        dma((NY, NG)), dma((NY, NG)), dma((NY, NG)), dma((NY, NG)),
    ]
    in_hbm = pl.BlockSpec(memory_space=pltpu.HBM)
    in_vmem = pl.BlockSpec(memory_space=pltpu.VMEM)
    mid = pl.pallas_call(
        functools.partial(block_kernel, C, F),
        out_shape=(
            jax.ShapeDtypeStruct((C, CAP, feat), BF16),
            jax.ShapeDtypeStruct((R, T), BF16),
            jax.ShapeDtypeStruct((rank, H), F32),
            jax.ShapeDtypeStruct((rank, feat), F32),
        ),
        in_specs=[in_hbm] * 10,
        out_specs=(in_vmem,) * 4,
        scratch_shapes=scratch,
        compiler_params=pltpu.CompilerParams(
            collective_id=0, has_side_effects=True, vmem_limit_bytes=52 * 2**20
        ),
    )(
        *(
            pltpu.with_memory_space_constraint(x, pltpu.HBM)
            for x in (
                tokens.T,
                cotangent.T,
                expert_indices.T,
                routing_weights.T,
                gate_up_weight_blocks[0],
                jnp.transpose(gate_up_block_scales[0], (2, 0, 1)),
                down_weight_blocks[0],
                jnp.transpose(down_block_scales, (2, 0, 1)),
                adapter_down_matrix[0].T,
                adapter_up_matrix[0],
            )
        )
    )
    out_t, left_t, right = pl.pallas_call(
        combine_kernel,
        out_shape=(
            jax.ShapeDtypeStruct((feat, T), BF16),
            jax.ShapeDtypeStruct((rank, H), F32),
            jax.ShapeDtypeStruct((rank, feat), F32),
        ),
        in_specs=[in_vmem] * 4,
        out_specs=(in_hbm,) * 3,
        scratch_shapes=[pltpu.VMEM((feat, T), BF16), dma((3,))],
        compiler_params=pltpu.CompilerParams(vmem_limit_bytes=16 * 2**20),
    )(*mid)
    return out_t.T, left_t.T[None], right[None]


def solution(mesh):
    placed = (
        P("ctx", "exp"),
        P("ctx", "exp"),
        P("ctx", None),
        P("ctx", None),
        P("ctx", None, "exp", None),
        P("ctx", None, "exp", None),
        P("ctx", "exp", None),
        P("ctx", "exp", None),
        P("ctx", "exp", None),
        P("ctx", None, "exp"),
    )
    return jax.shard_map(
        on_device,
        mesh=mesh,
        in_specs=placed,
        out_specs=(P("ctx", "exp"), P("ctx", "exp", None), P("ctx", None, "exp")),
        check_vma=False,
    )
```
